32 devices in a mesh: row: 4 (over y, core), col: 8 (over z, x).
Axes of the slice: x: 2, y: 2, z: 4, core: 2. Of those that a mesh axis runs over, the one named last changes fastest.
Arguments:
- row_points: bfloat16 [64, 1024], P(None, 'row'), may hold values from -6 to 6
- col_points: bfloat16 [64, 65536], P(None, 'col'), may hold values from -6 to 6
- random_panel: bfloat16 [65536, 128], P('col'), may hold values from -6 to 6
Outputs:
- left_basis: float32 [1024, 128], P('row')
- coefficients: bfloat16 [128, 65536], P('row', 'col')
The draws below stay inside these ranges and needn't reach their ends.
All inputs are finite; a program needn't handle non-finite values.
Results may differ from the reference program's by a relative error of at most 0.015.
Values may be sent and summed in bfloat16 or wider, within the bound.
No kernel may reach another device: no remote copies, remote signals or barrier semaphores. Data moves between devices by JAX's collectives and lax.ppermute only.
A program may use at most 64 MiB of HBM per device.

```python
import math
import jax
import jax.numpy as jnp
from jax import lax

DIM = 64
RANK = 128
ROWS = 1024
COLS = 65536


def block_scale(stream_key, extent, shards, smallest, high):
    def one(axis_at, blocks):
        heights = jax.random.uniform(jax.random.fold_in(jax.random.fold_in(stream_key, 6), axis_at), (blocks,), jnp.float32, smallest / len(shards), high / len(shards))
        return jnp.repeat(jnp.exp(heights), extent[axis_at] // blocks).reshape((-1,) + (1,) * (len(extent) - axis_at - 1))

    factor_of = one(*shards[0])
    for cut in shards[1:]:
        factor_of = factor_of * one(*cut)
    return factor_of


def noise(rng, extent, spread, limit, cuts=(), kind=jnp.bfloat16):
    level = block_scale(rng, extent, cuts, -0.22, 0.18) if cuts else 1.0
    entries = jax.random.normal(rng, extent, jnp.float32) * spread * level
    return jnp.minimum(jnp.maximum(entries, -limit), limit).astype(kind)


def setup_inputs(seed: int = 0) -> dict:
    key_of = jax.random.split(jax.random.key(seed), 4)
    return {
        "row_points": noise(key_of[0], (DIM, ROWS), 1.0, 6.0, ((1, 4),)),
        "col_points": noise(key_of[1], (DIM, COLS), 1.0, 6.0, ((1, 8),)),
        "random_panel": noise(key_of[2], (COLS, RANK), 1.0, 6.0, ((0, 8),)),
    }


def kernel_tile(points_left, left_sq, col_block):
    cross = jnp.dot(points_left.T.astype(jnp.float32), col_block.astype(jnp.float32), preferred_element_type=jnp.float32)
    col_sq = lax.optimization_barrier(jnp.sum(jnp.square(col_block.astype(jnp.float32)), axis=0))
    exp_scale = 2.0 / DIM
    return jnp.exp((2.0 * cross - left_sq[:, None] - col_sq[None, :]) * exp_scale)

def reference(row_points, col_points, random_panel):
    block_width = math.gcd(COLS, 4096)
    block_count = COLS // block_width
    row_sq = lax.optimization_barrier(jnp.sum(jnp.square(row_points.astype(jnp.float32)), axis=0))
    blocks = col_points.reshape(DIM, block_count, block_width).transpose(1, 0, 2)
    panel_blocks = random_panel.reshape(block_count, block_width, RANK)

    def add_block(accum_sum, block_pair):
        col_block, panel_block = block_pair
        kernel = kernel_tile(row_points, row_sq, col_block).astype(jnp.bfloat16)
        return (accum_sum + jnp.dot(kernel.astype(jnp.float32), panel_block.astype(jnp.float32), preferred_element_type=jnp.float32), None)
    sketch, _ = lax.scan(add_block, jnp.zeros((ROWS, RANK), jnp.float32), (blocks, panel_blocks))
    gram_matrix = jnp.dot(sketch.T.astype(jnp.float32), sketch.astype(jnp.float32), precision=lax.Precision.HIGHEST, preferred_element_type=jnp.float32)
    factor = jnp.linalg.cholesky(gram_matrix)
    orthonormal = jax.scipy.linalg.solve_triangular(factor, sketch.T, lower=True).T
    left_basis = orthonormal * math.sqrt(ROWS)
    orth_bf = orthonormal.astype(jnp.bfloat16)

    def project(col_block):
        kernel = kernel_tile(row_points, row_sq, col_block).astype(jnp.bfloat16)
        return jnp.dot(orth_bf.T.astype(jnp.float32), kernel.astype(jnp.float32), preferred_element_type=jnp.float32).astype(jnp.bfloat16)
    pieces = lax.map(project, blocks)
    coefficients = pieces.transpose(1, 0, 2).reshape(RANK, COLS)
    return (left_basis, coefficients)
```

```python
import functools
import math

import jax
import jax.numpy as jnp
from jax import lax
from jax.experimental import pallas as pl
from jax.experimental.pallas import tpu as pltpu
from jax.sharding import PartitionSpec as P

F32 = jnp.float32
BF16 = jnp.bfloat16
EXACT = lax.Precision.HIGHEST
VMEM_BYTES = 48 << 20


def contract(a, b, a_dim, b_dim, precision=None):
    dims = (((a_dim,), (b_dim,)), ((), ()))
    return lax.dot_general(a, b, dims, precision=precision, preferred_element_type=F32)


def widened(points, scale, factor, first):
    wide = points.astype(F32)
    terms_sum = -scale * jnp.sum(wide * wide, axis=0, keepdims=True)
    place = lax.broadcasted_iota(jnp.int32, (16, points.shape[1]), 0)
    terms_at, ones_at = (0, 3) if first else (3, 0)
    extra = jnp.where((place >= ones_at) & (place < ones_at + 3), 1.0, 0.0)
    for k in range(3):
        term = terms_sum.astype(BF16).astype(F32)
        extra = jnp.where(place == terms_at + k, term, extra)
        terms_sum = terms_sum - term
    return jnp.concatenate([(wide * factor).astype(BF16), extra.astype(BF16)], axis=0)


def kernel_values(left, col_points, scale):
    return jnp.exp(contract(left, widened(col_points, scale, 1.0, False), 1, 0)).astype(BF16)


def sketch_body(scale, chunk, row_ref, col_ref, panel_ref, half_ref, keep_ref, send_ref, total_ref):
    left = widened(row_ref[...], scale, 2.0 * scale, True).T
    total = jnp.zeros(total_ref.shape, F32)
    for c in range(0, col_ref.shape[1], chunk):
        tile = kernel_values(left, col_ref[:, c : c + chunk], scale)
        total = total + contract(tile, panel_ref[c : c + chunk, :], 1, 0)
    total_ref[...] = total
    half, rows = half_ref[0], keep_ref.shape[0]
    keep_ref[...] = total_ref[pl.ds(pl.multiple_of(half * rows, rows), rows), :]
    send_ref[...] = total_ref[pl.ds(pl.multiple_of((1 - half) * rows, rows), rows), :]


def sketch_halves(row_points, col_points, panel, half):
    dim, rows = row_points.shape
    col_dev, width = panel.shape
    part = jax.ShapeDtypeStruct((rows // 2, width), F32)
    whole = pl.BlockSpec(memory_space=pltpu.VMEM)
    return pl.pallas_call(
        functools.partial(sketch_body, 2.0 / dim, math.gcd(col_dev, 1024)),
        in_specs=[whole, whole, whole, pl.BlockSpec(memory_space=pltpu.SMEM)],
        out_specs=[whole, whole],
        out_shape=[part, part],
        scratch_shapes=[pltpu.VMEM((rows, width), F32)],
        compiler_params=pltpu.CompilerParams(vmem_limit_bytes=VMEM_BYTES),
        name="sketch",
    )(row_points, col_points, panel, half)


def inverse_factor(gram):
    n = gram.shape[0]
    tiles = n // 8
    left = [gram[8 * t : 8 * t + 8, :] for t in range(tiles)]
    lane = lax.broadcasted_iota(jnp.int32, (8, n), 1)
    sub = lax.broadcasted_iota(jnp.int32, (8, n), 0)
    right = [jnp.where(lane == sub + 8 * t, 1.0, 0.0) for t in range(tiles)]
    inverse = []

    def row(tile, k):
        return jnp.broadcast_to(tile[k : k + 1, :], (8, n))

    def column(tile, k):
        return jnp.broadcast_to(tile[:, k : k + 1], (8, n))

    def weighted(weights, rows):
        pairs = [w * r for w, r in zip(weights, rows)]
        while len(pairs) > 1:
            pairs = [a + b for a, b in zip(pairs[::2], pairs[1::2])]
        return pairs[0]

    for b in range(tiles):
        upper, lower = left[b], right[b]
        block = [column(upper, 8 * b + k) for k in range(8)]
        root, below = [], []
        for k in range(8):
            root.append(lax.rsqrt(row(block[k], k)))
            step = jnp.where(sub > k, block[k] * root[k], 0.0)
            below.append({j: row(step, j) for j in range(k + 1, 8)})
            for j in range(k + 1, 8):
                block[j] = block[j] - step * below[k][j]
            upper_row, lower_row = row(upper, k) * root[k], row(lower, k) * root[k]
            upper, lower = upper - step * upper_row, lower - step * lower_row
        scales = root[0]
        for k in range(1, 8):
            scales = jnp.where(sub == k, root[k], scales)
        upper, lower = upper * scales, lower * scales
        inverse.append(lower)
        upper_rows = [row(upper, k) for k in range(8)]
        lower_rows = [row(lower, k) for k in range(8)]
        for t in range(b + 1, tiles):
            entry = [column(left[t], 8 * b + k) for k in range(8)]
            for k in range(8):
                entry[k] = entry[k] * root[k]
                for j in range(k + 1, 8):
                    entry[j] = entry[j] - entry[k] * below[k][j]
            left[t] = left[t] - weighted(entry, upper_rows)
            right[t] = right[t] - weighted(entry, lower_rows)
    return inverse


def factor_body(norm, rank_ref, sketch_ref, left_basis_ref, ranks_ref, inverse_ref):
    sketch = sketch_ref[...]
    gram = contract(sketch, sketch, 0, 0, EXACT)
    for t, tile in enumerate(inverse_factor(gram)):
        inverse_ref[8 * t : 8 * t + 8, :] = tile
    own = sketch_ref[: left_basis_ref.shape[0], :]
    left_basis_ref[...] = contract(own, inverse_ref[...], 1, 1, EXACT) * norm
    count = ranks_ref.shape[0]
    mine = inverse_ref[pl.ds(pl.multiple_of(rank_ref[0] * count, count), count), :]
    ranks_ref[...] = contract(mine, sketch, 1, 1, EXACT).astype(BF16)


def factor(sketch, rows, share, index):
    total, width = sketch.shape
    whole = pl.BlockSpec(memory_space=pltpu.VMEM)
    return pl.pallas_call(
        functools.partial(factor_body, math.sqrt(total)),
        in_specs=[pl.BlockSpec(memory_space=pltpu.SMEM), whole],
        out_specs=[whole, whole],
        out_shape=[jax.ShapeDtypeStruct((rows, width), F32), jax.ShapeDtypeStruct((share, total), BF16)],
        scratch_shapes=[pltpu.VMEM((width, width), F32)],
        compiler_params=pltpu.CompilerParams(vmem_limit_bytes=VMEM_BYTES),
        name="factor",
    )(index, sketch)


def project_body(scale, chunk, ranks_ref, row_ref, col_ref, out_ref, left_ref):
    @pl.when(pl.program_id(0) == 0)
    def _():
        rows = row_ref.shape[2]
        for k in range(row_ref.shape[0]):
            left_ref[k * rows : (k + 1) * rows, :] = widened(row_ref[k], scale, 2.0 * scale, True).T

    ranks = ranks_ref[...]
    for c in range(0, col_ref.shape[1], chunk):
        tile = kernel_values(left_ref[...], col_ref[:, c : c + chunk], scale)
        out_ref[:, c : c + chunk] = contract(ranks, tile, 1, 0).astype(BF16)


def project(ranks, row_blocks, col_points):
    count, total = ranks.shape
    blocks, dim, rows = row_blocks.shape
    col_dev = col_points.shape[1]
    width = math.gcd(col_dev, 2048)
    return pl.pallas_call(
        functools.partial(project_body, 2.0 / dim, math.gcd(width, 512)),
        grid=(col_dev // width,),
        in_specs=[
            pl.BlockSpec((count, total), lambda i: (0, 0)),
            pl.BlockSpec((blocks, dim, rows), lambda i: (0, 0, 0)),
            pl.BlockSpec((dim, width), lambda i: (0, i)),
        ],
        out_specs=pl.BlockSpec((count, width), lambda i: (0, i)),
        out_shape=jax.ShapeDtypeStruct((count, col_dev), BF16),
        scratch_shapes=[pltpu.VMEM((total, dim + 16), BF16)],
        compiler_params=pltpu.CompilerParams(vmem_limit_bytes=VMEM_BYTES),
        name="project",
    )(ranks, row_blocks, col_points)


def swapped(value, axis, bit):
    return lax.ppermute(value, axis, [(i, i ^ bit) for i in range(lax.axis_size(axis))])


def bits_down(size):
    return [1 << k for k in reversed(range(size.bit_length() - 1))]


def per_device(row_points, col_points, random_panel):
    rows = row_points.shape[1]
    width = random_panel.shape[1]
    row_count, col_count = lax.axis_size("row"), lax.axis_size("col")
    row_at, col_at = lax.axis_index("row"), lax.axis_index("col")

    row_blocks = row_points[None]
    for bit in bits_down(row_count):
        row_blocks = jnp.concatenate([row_blocks, swapped(row_blocks, "row", bit)], axis=0)

    half = col_at % 2
    keep, send = sketch_halves(row_points, col_points, random_panel, half.reshape(1))
    part = keep + swapped(send, "col", 1)
    for bit in reversed(bits_down(col_count)[:-1]):
        part = part + swapped(part, "col", bit)
    other = swapped(part, "col", 1)
    first = half == 0
    sketch = jnp.concatenate([jnp.where(first, part, other), jnp.where(first, other, part)], axis=0)
    for bit in bits_down(row_count):
        sketch = jnp.concatenate([sketch, swapped(sketch, "row", bit)], axis=0)

    left_basis, ranks = factor(sketch, rows, width // row_count, row_at.reshape(1))
    return (left_basis, project(ranks, row_blocks, col_points))


def solution(mesh):
    placed = (P(None, "row"), P(None, "col"), P("col", None))
    return jax.shard_map(
        per_device,
        mesh=mesh,
        in_specs=placed,
        out_specs=(P("row", None), P("row", "col")),
        check_vma=False,
    )
```

```python
import functools
import math

import jax
import jax.numpy as jnp
from jax import lax
from jax.experimental import pallas as pl
from jax.experimental.pallas import tpu as pltpu
from jax.sharding import PartitionSpec as P

F32 = jnp.float32
BF16 = jnp.bfloat16
EXACT = lax.Precision.HIGHEST
VMEM_BYTES = 24 << 20
TILE_BYTES = 16 << 20


def contract(a, b, a_dim, b_dim, precision=None):
    dims = (((a_dim,), (b_dim,)), ((), ()))
    return lax.dot_general(a, b, dims, precision=precision, preferred_element_type=F32)


def widened(points, scale, factor, first):
    wide = points.astype(F32)
    terms_sum = -scale * jnp.sum(wide * wide, axis=0, keepdims=True)
    place = lax.broadcasted_iota(jnp.int32, (16, points.shape[1]), 0)
    terms_at, ones_at = (0, 3) if first else (3, 0)
    extra = jnp.where((place >= ones_at) & (place < ones_at + 3), 1.0, 0.0)
    for k in range(3):
        term = terms_sum.astype(BF16).astype(F32)
        extra = jnp.where(place == terms_at + k, term, extra)
        terms_sum = terms_sum - term
    return jnp.concatenate([(wide * factor).astype(BF16), extra.astype(BF16)], axis=0)


def exponent(left, right):
    return jnp.exp(contract(left, right, 1, 0)).astype(BF16)


def chunk_width(col_dev):
    return math.gcd(col_dev, 1024)


def sketch_body(
    scale, half_ref, row_hbm, col_hbm, panel_hbm, keep_ref, send_ref, tile_ref, right_ref,
    row_ref, col_ref, panel_ref, total_ref, row_sem, col_sem, panel_sem,
):
    chunk = chunk_width(col_hbm.shape[1])
    count = col_hbm.shape[1] // chunk
    row_copy = pltpu.make_async_copy(row_hbm, row_ref, row_sem)
    row_copy.start()
    col_copies, panel_copies = [], []
    for k in range(count):
        at = slice(k * chunk, (k + 1) * chunk)
        col_copies.append(pltpu.make_async_copy(col_hbm.at[:, at], col_ref.at[:, at], col_sem.at[k]))
        panel_copies.append(pltpu.make_async_copy(panel_hbm.at[at, :], panel_ref.at[at, :], panel_sem.at[k]))
        col_copies[k].start()
        panel_copies[k].start()
    row_copy.wait()
    left = widened(row_ref[...], scale, 2.0 * scale, True).T
    total = jnp.zeros(total_ref.shape, F32)
    for k in range(count):
        at = slice(k * chunk, (k + 1) * chunk)
        col_copies[k].wait()
        right = widened(col_ref[:, at], scale, 1.0, False)
        right_ref[:, at] = right
        tile = exponent(left, right)
        tile_ref[:, at] = tile
        panel_copies[k].wait()
        total = total + contract(tile, panel_ref[at, :], 1, 0)
    total_ref[...] = total
    half, rows = half_ref[0], keep_ref.shape[0]
    keep_ref[...] = total_ref[pl.ds(pl.multiple_of(half * rows, rows), rows), :]
    send_ref[...] = total_ref[pl.ds(pl.multiple_of((1 - half) * rows, rows), rows), :]


def sketch_halves(row_points, col_points, panel, half):
    dim, rows = row_points.shape
    col_dev, width = panel.shape
    count = col_dev // chunk_width(col_dev)
    part = jax.ShapeDtypeStruct((rows // 2, width), F32)
    whole, remote = pl.BlockSpec(memory_space=pltpu.VMEM), pl.BlockSpec(memory_space=pltpu.HBM)
    return pl.pallas_call(
        functools.partial(sketch_body, 2.0 / dim),
        in_specs=[pl.BlockSpec(memory_space=pltpu.SMEM), remote, remote, remote],
        out_specs=[whole] * 4,
        out_shape=[
            part,
            part,
            jax.ShapeDtypeStruct((rows, col_dev), BF16),
            jax.ShapeDtypeStruct((dim + 16, col_dev), BF16),
        ],
        scratch_shapes=[
            pltpu.VMEM((dim, rows), BF16),
            pltpu.VMEM((dim, col_dev), BF16),
            pltpu.VMEM((col_dev, width), BF16),
            pltpu.VMEM((rows, width), F32),
            pltpu.SemaphoreType.DMA,
            pltpu.SemaphoreType.DMA((count,)),
            pltpu.SemaphoreType.DMA((count,)),
        ],
        compiler_params=pltpu.CompilerParams(vmem_limit_bytes=VMEM_BYTES),
        name="sketch",
    )(half, *[pltpu.with_memory_space_constraint(a, pltpu.HBM) for a in (row_points, col_points, panel)])


def tile_body(scale, row_ref, right_ref, tile_ref):
    left = widened(row_ref[...], scale, 2.0 * scale, True).T
    chunk = chunk_width(right_ref.shape[1])
    for c in range(0, right_ref.shape[1], chunk):
        tile_ref[:, c : c + chunk] = exponent(left, right_ref[:, c : c + chunk])


def kernel_tile(row_points, right):
    dim, rows = row_points.shape
    depth, col_dev = right.shape
    whole = pl.BlockSpec(memory_space=pltpu.VMEM)
    return pl.pallas_call(
        functools.partial(tile_body, 2.0 / dim),
        in_specs=[whole, whole],
        out_specs=whole,
        out_shape=jax.ShapeDtypeStruct((rows, col_dev), BF16),
        compiler_params=pltpu.CompilerParams(vmem_limit_bytes=VMEM_BYTES),
        cost_estimate=pl.CostEstimate(
            flops=2 * rows * depth * col_dev,
            bytes_accessed=2 * (rows + depth) * col_dev,
            transcendentals=rows * col_dev,
        ),
        name="kernel_tile",
    )(row_points, right)


def inverse_factor(gram):
    n = gram.shape[0]
    tiles = n // 8
    left = [gram[8 * t : 8 * t + 8, :] for t in range(tiles)]
    lane = lax.broadcasted_iota(jnp.int32, (8, n), 1)
    sub = lax.broadcasted_iota(jnp.int32, (8, n), 0)
    right = [jnp.where(lane == sub + 8 * t, 1.0, 0.0) for t in range(tiles)]
    inverse = []

    def row(tile, k):
        return jnp.broadcast_to(tile[k : k + 1, :], (8, n))

    def column(tile, k):
        return jnp.broadcast_to(tile[:, k : k + 1], (8, n))

    def weighted(weights, rows):
        pairs = [w * r for w, r in zip(weights, rows)]
        while len(pairs) > 1:
            pairs = [a + b for a, b in zip(pairs[::2], pairs[1::2])]
        return pairs[0]

    for b in range(tiles):
        upper, lower = left[b], right[b]
        block = [column(upper, 8 * b + k) for k in range(8)]
        root, below = [], []
        for k in range(8):
            root.append(lax.rsqrt(row(block[k], k)))
            step = jnp.where(sub > k, block[k] * root[k], 0.0)
            below.append({j: row(step, j) for j in range(k + 1, 8)})
            for j in range(k + 1, 8):
                block[j] = block[j] - step * below[k][j]
            upper_row, lower_row = row(upper, k) * root[k], row(lower, k) * root[k]
            upper, lower = upper - step * upper_row, lower - step * lower_row
        scales = root[0]
        for k in range(1, 8):
            scales = jnp.where(sub == k, root[k], scales)
        upper, lower = upper * scales, lower * scales
        inverse.append(lower)
        upper_rows = [row(upper, k) for k in range(8)]
        lower_rows = [row(lower, k) for k in range(8)]
        for t in range(b + 1, tiles):
            entry = [column(left[t], 8 * b + k) for k in range(8)]
            for k in range(8):
                entry[k] = entry[k] * root[k]
                for j in range(k + 1, 8):
                    entry[j] = entry[j] - entry[k] * below[k][j]
            left[t] = left[t] - weighted(entry, upper_rows)
            right[t] = right[t] - weighted(entry, lower_rows)
    return inverse


def factor_body(norm, rank_ref, sketch_ref, left_basis_ref, ranks_ref, inverse_ref):
    sketch = sketch_ref[...]
    gram = contract(sketch, sketch, 0, 0, EXACT)
    for t, tile in enumerate(inverse_factor(gram)):
        inverse_ref[8 * t : 8 * t + 8, :] = tile
    own = sketch_ref[: left_basis_ref.shape[0], :]
    left_basis_ref[...] = contract(own, inverse_ref[...], 1, 1, EXACT) * norm
    count = ranks_ref.shape[0]
    mine = inverse_ref[pl.ds(pl.multiple_of(rank_ref[0] * count, count), count), :]
    ranks_ref[...] = contract(mine, sketch, 1, 1, EXACT).astype(BF16)


def factor(sketch, rows, share, index):
    total, width = sketch.shape
    whole = pl.BlockSpec(memory_space=pltpu.VMEM)
    return pl.pallas_call(
        functools.partial(factor_body, math.sqrt(total)),
        in_specs=[pl.BlockSpec(memory_space=pltpu.SMEM), whole],
        out_specs=[whole, whole],
        out_shape=[jax.ShapeDtypeStruct((rows, width), F32), jax.ShapeDtypeStruct((share, total), BF16)],
        scratch_shapes=[pltpu.VMEM((width, width), F32)],
        compiler_params=pltpu.CompilerParams(vmem_limit_bytes=VMEM_BYTES),
        name="factor",
    )(index, sketch)


def project_body(ranks_ref, *refs):
    *tile_refs, out_ref = refs
    chunk = chunk_width(out_ref.shape[1])
    rows = tile_refs[0].shape[0]
    for c in range(0, out_ref.shape[1], chunk):
        total = None
        for k, tile_ref in enumerate(tile_refs):
            piece = contract(ranks_ref[:, k * rows : (k + 1) * rows], tile_ref[:, c : c + chunk], 1, 0)
            total = piece if total is None else total + piece
        out_ref[:, c : c + chunk] = total.astype(BF16)


def project(ranks, tiles):
    whole = pl.BlockSpec(memory_space=pltpu.VMEM)
    return pl.pallas_call(
        project_body,
        in_specs=[whole] * (1 + len(tiles)),
        out_specs=whole,
        out_shape=jax.ShapeDtypeStruct((ranks.shape[0], tiles[0].shape[1]), BF16),
        compiler_params=pltpu.CompilerParams(vmem_limit_bytes=VMEM_BYTES),
        name="project",
    )(ranks, *tiles)


def project_anew_body(scale, ranks_ref, row_ref, right_ref, out_ref, left_ref):
    @pl.when(pl.program_id(0) == 0)
    def _():
        rows = row_ref.shape[2]
        for k in range(row_ref.shape[0]):
            left_ref[k * rows : (k + 1) * rows, :] = widened(row_ref[k], scale, 2.0 * scale, True).T

    out_ref[...] = contract(ranks_ref[...], exponent(left_ref[...], right_ref[...]), 1, 0).astype(BF16)


def project_anew(ranks, row_blocks, right):
    count, total = ranks.shape
    blocks, dim, rows = row_blocks.shape
    depth, col_dev = right.shape
    width = math.gcd(col_dev, 512)
    return pl.pallas_call(
        functools.partial(project_anew_body, 2.0 / dim),
        grid=(col_dev // width,),
        in_specs=[
            pl.BlockSpec((count, total), lambda i: (0, 0)),
            pl.BlockSpec((blocks, dim, rows), lambda i: (0, 0, 0)),
            pl.BlockSpec((depth, width), lambda i: (0, i)),
        ],
        out_specs=pl.BlockSpec((count, width), lambda i: (0, i)),
        out_shape=jax.ShapeDtypeStruct((count, col_dev), BF16),
        scratch_shapes=[pltpu.VMEM((total, depth), BF16)],
        compiler_params=pltpu.CompilerParams(vmem_limit_bytes=VMEM_BYTES),
        name="project_anew",
    )(ranks, row_blocks, right)


def swapped(value, row_bit, col_bit):
    rows, cols = lax.axis_size("row"), lax.axis_size("col")
    pairs = [(r * cols + c, (r ^ row_bit) * cols + (c ^ col_bit)) for r in range(rows) for c in range(cols)]
    return lax.ppermute(value, ("row", "col"), pairs)


def bits_down(size):
    return [1 << k for k in reversed(range(size.bit_length() - 1))]


def per_device(row_points, col_points, random_panel):
    rows = row_points.shape[1]
    col_dev, width = random_panel.shape
    row_count, col_count = lax.axis_size("row"), lax.axis_size("col")
    row_at, col_at = lax.axis_index("row"), lax.axis_index("col")
    half = col_at % 2
    keep, send, tile, right = sketch_halves(row_points, col_points, random_panel, half.reshape(1))
    tiles = [tile]
    fits = row_count * rows * col_dev * 2 <= TILE_BYTES

    part = keep + swapped(send, 0, 1)
    blocks = [lax.optimization_barrier((row_points, keep))[0]]
    for bit in bits_down(row_count):
        blocks = blocks + [swapped(block, bit, 0) for block in blocks]

    def beside(transferred):
        if not fits or len(tiles) == row_count:
            return transferred
        transferred, tile = lax.optimization_barrier((transferred, kernel_tile(blocks[len(tiles)], right)))
        tiles.append(tile)
        return transferred

    for bit in reversed(bits_down(col_count)[:-1]):
        part = part + beside(swapped(part, 0, bit))

    row_bits = bits_down(row_count)
    first = half == 0

    def ordered(mine, other):
        return jnp.concatenate([jnp.where(first, mine, other), jnp.where(first, other, mine)], axis=0)

    bit = row_bits[0]
    moved = beside((swapped(part, 0, 1), swapped(part, bit, 0), swapped(part, bit, 1)))
    sketch = jnp.concatenate([ordered(part, moved[0]), ordered(moved[1], moved[2])], axis=0)
    for bit in row_bits[1:]:
        sketch = jnp.concatenate([sketch, swapped(sketch, bit, 0)], axis=0)

    left_basis, ranks = factor(sketch, rows, width // row_count, row_at.reshape(1))
    if fits:
        while len(tiles) < row_count:
            tiles.append(kernel_tile(blocks[len(tiles)], right))
        return (left_basis, project(ranks, tiles))
    return (left_basis, project_anew(ranks, jnp.stack(blocks), right))


def solution(mesh):
    placed = (P(None, "row"), P(None, "col"), P("col", None))
    return jax.shard_map(
        per_device,
        mesh=mesh,
        in_specs=placed,
        out_specs=(P("row", None), P("row", "col")),
        check_vma=False,
    )
```

```python
import functools
import math

import jax
import jax.numpy as jnp
from jax import lax
from jax.experimental import pallas as pl
from jax.experimental.pallas import tpu as pltpu
from jax.sharding import PartitionSpec as P

F32 = jnp.float32
BF16 = jnp.bfloat16
EXACT = lax.Precision.HIGHEST
VMEM_BYTES = 40 << 20
TILE_BYTES = 16 << 20


def contract(a, b, a_dim, b_dim, precision=None):
    dims = (((a_dim,), (b_dim,)), ((), ()))
    return lax.dot_general(a, b, dims, precision=precision, preferred_element_type=F32)


def widened(points, scale, factor, first):
    wide = points.astype(F32)
    terms_sum = -scale * jnp.sum(wide * wide, axis=0, keepdims=True)
    place = lax.broadcasted_iota(jnp.int32, (16, points.shape[1]), 0)
    terms_at, ones_at = (0, 3) if first else (3, 0)
    extra = jnp.where((place >= ones_at) & (place < ones_at + 3), 1.0, 0.0)
    for k in range(3):
        term = terms_sum.astype(BF16).astype(F32)
        extra = jnp.where(place == terms_at + k, term, extra)
        terms_sum = terms_sum - term
    return jnp.concatenate([(wide * factor).astype(BF16), extra.astype(BF16)], axis=0)


def exponent(left, right):
    return jnp.exp(contract(left, right, 1, 0)).astype(BF16)


def chunk_width(col_dev):
    return math.gcd(col_dev, 1024)


def sketch_body(
    scale, half_ref, row_hbm, col_hbm, panel_hbm, keep_ref, send_ref,
    row_ref, col_ref, panel_ref, tile_ref, total_ref, row_sem, col_sem, panel_sem,
):
    row_copy = pltpu.make_async_copy(row_hbm, row_ref, row_sem)
    col_copy = pltpu.make_async_copy(col_hbm, col_ref, col_sem)
    panel_copy = pltpu.make_async_copy(panel_hbm, panel_ref, panel_sem)
    row_copy.start()
    col_copy.start()
    panel_copy.start()
    chunk = chunk_width(col_ref.shape[1])
    row_copy.wait()
    left = widened(row_ref[...], scale, 2.0 * scale, True).T
    col_copy.wait()
    for c in range(0, col_ref.shape[1], chunk):
        right = widened(col_ref[:, c : c + chunk], scale, 1.0, False)
        tile_ref[:, c : c + chunk] = exponent(left, right)
    panel_copy.wait()
    total_ref[...] = contract(tile_ref[...], panel_ref[...], 1, 0)
    half, rows = half_ref[0], keep_ref.shape[0]
    keep_ref[...] = total_ref[pl.ds(pl.multiple_of(half * rows, rows), rows), :]
    send_ref[...] = total_ref[pl.ds(pl.multiple_of((1 - half) * rows, rows), rows), :]


def sketch_halves(row_points, col_points, panel, half):
    dim, rows = row_points.shape
    col_dev, width = panel.shape
    part = jax.ShapeDtypeStruct((rows // 2, width), F32)
    whole, remote = pl.BlockSpec(memory_space=pltpu.VMEM), pl.BlockSpec(memory_space=pltpu.HBM)
    return pl.pallas_call(
        functools.partial(sketch_body, 2.0 / dim),
        in_specs=[pl.BlockSpec(memory_space=pltpu.SMEM), remote, remote, remote],
        out_specs=[whole, whole],
        out_shape=[part, part],
        scratch_shapes=[
            pltpu.VMEM((dim, rows), BF16),
            pltpu.VMEM((dim, col_dev), BF16),
            pltpu.VMEM((col_dev, width), BF16),
            pltpu.VMEM((rows, col_dev), BF16),
            pltpu.VMEM((rows, width), F32),
            pltpu.SemaphoreType.DMA,
            pltpu.SemaphoreType.DMA,
            pltpu.SemaphoreType.DMA,
        ],
        compiler_params=pltpu.CompilerParams(vmem_limit_bytes=VMEM_BYTES),
        name="sketch",
    )(half, *[pltpu.with_memory_space_constraint(a, pltpu.HBM) for a in (row_points, col_points, panel)])


def inverse_factor(gram, after_step):
    n = gram.shape[0]
    tiles = n // 8
    left = [gram[8 * t : 8 * t + 8, :] for t in range(tiles)]
    lane = lax.broadcasted_iota(jnp.int32, (8, n), 1)
    sub = lax.broadcasted_iota(jnp.int32, (8, n), 0)
    right = [jnp.where(lane == sub + 8 * t, 1.0, 0.0) for t in range(tiles)]
    inverse = []

    def row(tile, k):
        return jnp.broadcast_to(tile[k : k + 1, :], (8, n))

    def column(tile, k):
        return jnp.broadcast_to(tile[:, k : k + 1], (8, n))

    def weighted(weights, rows):
        pairs = [w * r for w, r in zip(weights, rows)]
        while len(pairs) > 1:
            pairs = [a + b for a, b in zip(pairs[::2], pairs[1::2])]
        return pairs[0]

    for b in range(tiles):
        upper, lower = left[b], right[b]
        block = [column(upper, 8 * b + k) for k in range(8)]
        root, below = [], []
        for k in range(8):
            root.append(lax.rsqrt(row(block[k], k)))
            step = jnp.where(sub > k, block[k] * root[k], 0.0)
            below.append({j: row(step, j) for j in range(k + 1, 8)})
            for j in range(k + 1, 8):
                block[j] = block[j] - step * below[k][j]
            upper_row, lower_row = row(upper, k) * root[k], row(lower, k) * root[k]
            upper, lower = upper - step * upper_row, lower - step * lower_row
        scales = root[0]
        for k in range(1, 8):
            scales = jnp.where(sub == k, root[k], scales)
        upper, lower = upper * scales, lower * scales
        inverse.append(lower)
        after_step((b + 1) / tiles)
        upper_rows = [row(upper, k) for k in range(8)]
        lower_rows = [row(lower, k) for k in range(8)]
        for t in range(b + 1, tiles):
            entry = [column(left[t], 8 * b + k) for k in range(8)]
            for k in range(8):
                entry[k] = entry[k] * root[k]
                for j in range(k + 1, 8):
                    entry[j] = entry[j] - entry[k] * below[k][j]
            left[t] = left[t] - weighted(entry, upper_rows)
            right[t] = right[t] - weighted(entry, lower_rows)
    return inverse


def finish_body(
    scale, norm, stored, rank_ref, sketch_ref, row_ref, col_ref, left_basis_ref, out_ref, inverse_ref, left_ref, tile_ref
):
    blocks, _, rows = row_ref.shape
    total, col_dev = left_ref.shape[0], col_ref.shape[1]
    chunk = tile_ref.shape[1] if not stored else chunk_width(col_dev) // 2
    sketch = sketch_ref[...]
    gram = contract(sketch, sketch, 0, 0, EXACT)
    for k in range(blocks):
        left_ref[k * rows : (k + 1) * rows, :] = widened(row_ref[k], scale, 2.0 * scale, True).T
    work = [(k, c) for c in range(0, col_dev, chunk) for k in range(blocks)] if stored else []
    done = 0

    def tiles_until(share):
        nonlocal done
        upto = int(len(work) * share)
        for k, c in work[done:upto]:
            at = slice(k * rows, (k + 1) * rows)
            right = widened(col_ref[:, c : c + chunk], scale, 1.0, False)
            tile_ref[at, c : c + chunk] = exponent(left_ref[at, :], right)
        done = upto

    for t, tile in enumerate(inverse_factor(gram, tiles_until)):
        inverse_ref[8 * t : 8 * t + 8, :] = tile
    left_basis_ref[...] = contract(sketch_ref[:rows, :], inverse_ref[...], 1, 1, EXACT) * norm
    count = out_ref.shape[0]
    mine = inverse_ref[pl.ds(pl.multiple_of(rank_ref[0] * count, count), count), :]
    ranks = contract(mine, sketch_ref[...], 1, 1, EXACT).astype(BF16)
    if stored:
        for c in range(0, col_dev, 2 * chunk):
            at = slice(c, c + 2 * chunk)
            out_ref[:, at] = contract(ranks, tile_ref[:, at], 1, 0).astype(BF16)
    else:

        @pl.loop(0, col_dev // chunk)
        def _(k):
            at = pl.ds(pl.multiple_of(k * chunk, chunk), chunk)
            tile_ref[...] = exponent(left_ref[...], widened(col_ref[:, at], scale, 1.0, False))
            out_ref[:, at] = contract(ranks, tile_ref[...], 1, 0).astype(BF16)


def finish(index, sketch, row_blocks, col_points):
    total, width = sketch.shape
    blocks, dim, rows = row_blocks.shape
    col_dev = col_points.shape[1]
    stored = total * col_dev * 2 <= TILE_BYTES
    count = width // blocks
    whole = pl.BlockSpec(memory_space=pltpu.VMEM)
    return pl.pallas_call(
        functools.partial(finish_body, 2.0 / dim, math.sqrt(total), stored),
        in_specs=[pl.BlockSpec(memory_space=pltpu.SMEM), whole, whole, whole],
        out_specs=[whole, whole],
        out_shape=[jax.ShapeDtypeStruct((rows, width), F32), jax.ShapeDtypeStruct((count, col_dev), BF16)],
        scratch_shapes=[
            pltpu.VMEM((width, width), F32),
            pltpu.VMEM((total, dim + 16), BF16),
            pltpu.VMEM((total, col_dev if stored else math.gcd(col_dev, 512)), BF16),
        ],
        compiler_params=pltpu.CompilerParams(vmem_limit_bytes=VMEM_BYTES),
        name="finish",
    )(index, sketch, row_blocks, col_points)


def swapped(value, row_bit, col_bit):
    rows, cols = lax.axis_size("row"), lax.axis_size("col")
    pairs = [(r * cols + c, (r ^ row_bit) * cols + (c ^ col_bit)) for r in range(rows) for c in range(cols)]
    return lax.ppermute(value, ("row", "col"), pairs)


def bits_down(size):
    return [1 << k for k in reversed(range(size.bit_length() - 1))]


def per_device(row_points, col_points, random_panel):
    row_count, col_count = lax.axis_size("row"), lax.axis_size("col")
    half = lax.axis_index("col") % 2
    row_bits, col_bits = bits_down(row_count), bits_down(col_count)
    keep, send = sketch_halves(row_points, col_points, random_panel, half.reshape(1))

    def both(blocks, moved):
        return jnp.concatenate([blocks, moved], axis=0)

    first = half == 0
    row_blocks = lax.optimization_barrier((row_points, keep))[0][None]
    moved = (swapped(send, 0, 1), swapped(row_blocks, row_bits[0], 0))
    moved_part, moved_blocks = lax.optimization_barrier(moved)
    part, row_blocks = keep + moved_part, both(row_blocks, moved_blocks)
    for bit in reversed(col_bits[:-1]):
        part = part + swapped(part, 0, bit)

    def ordered(mine, other):
        return both(jnp.where(first, mine, other), jnp.where(first, other, mine))

    bit = row_bits[0]
    near, far, cross = swapped(part, 0, 1), swapped(part, bit, 0), swapped(part, bit, 1)
    sketch = both(ordered(part, near), ordered(far, cross))
    for bit in row_bits[1:]:
        sketch, row_blocks = [both(a, swapped(a, bit, 0)) for a in (sketch, row_blocks)]
    return finish(lax.axis_index("row").reshape(1), sketch, row_blocks, col_points)


def solution(mesh):
    placed = (P(None, "row"), P(None, "col"), P("col", None))
    return jax.shard_map(
        per_device,
        mesh=mesh,
        in_specs=placed,
        out_specs=(P("row", None), P("row", "col")),
        check_vma=False,
    )
```

```python
import functools
import math

import jax
import jax.numpy as jnp
from jax import lax
from jax.experimental import pallas as pl
from jax.experimental.pallas import tpu as pltpu
from jax.sharding import PartitionSpec as P

F32 = jnp.float32
BF16 = jnp.bfloat16
EXACT = lax.Precision.HIGHEST
VMEM_BYTES = 40 << 20
TILE_BYTES = 16 << 20


def contract(a, b, a_dim, b_dim, precision=None):
    dims = (((a_dim,), (b_dim,)), ((), ()))
    return lax.dot_general(a, b, dims, precision=precision, preferred_element_type=F32)


def widened(points, scale, factor, first):
    wide = points.astype(F32)
    terms_sum = -scale * jnp.sum(wide * wide, axis=0, keepdims=True)
    place = lax.broadcasted_iota(jnp.int32, (16, points.shape[1]), 0)
    terms_at, ones_at = (0, 3) if first else (3, 0)
    extra = jnp.where((place >= ones_at) & (place < ones_at + 3), 1.0, 0.0)
    for k in range(3):
        term = terms_sum.astype(BF16).astype(F32)
        extra = jnp.where(place == terms_at + k, term, extra)
        terms_sum = terms_sum - term
    return jnp.concatenate([(wide * factor).astype(BF16), extra.astype(BF16)], axis=0)


def exponent(left, right):
    return jnp.exp(contract(left, right, 1, 0)).astype(BF16)


def chunk_width(col_dev):
    return math.gcd(col_dev, 1024)


def sketch_body(
    scale, half_ref, row_hbm, col_hbm, panel_hbm, keep_ref, send_ref,
    row_ref, col_ref, panel_ref, tile_ref, total_ref, row_sem, col_sem, panel_sem,
):
    row_copy = pltpu.make_async_copy(row_hbm, row_ref, row_sem)
    col_copy = pltpu.make_async_copy(col_hbm, col_ref, col_sem)
    panel_copy = pltpu.make_async_copy(panel_hbm, panel_ref, panel_sem)
    row_copy.start()
    col_copy.start()
    panel_copy.start()
    chunk = chunk_width(col_ref.shape[1])
    row_copy.wait()
    left = widened(row_ref[...], scale, 2.0 * scale, True).T
    col_copy.wait()
    for c in range(0, col_ref.shape[1], chunk):
        right = widened(col_ref[:, c : c + chunk], scale, 1.0, False)
        tile_ref[:, c : c + chunk] = exponent(left, right)
    panel_copy.wait()
    total_ref[...] = contract(tile_ref[...], panel_ref[...], 1, 0)
    half, rows = half_ref[0], keep_ref.shape[0]
    keep_ref[...] = total_ref[pl.ds(pl.multiple_of(half * rows, rows), rows), :]
    send_ref[...] = total_ref[pl.ds(pl.multiple_of((1 - half) * rows, rows), rows), :]


def sketch_halves(row_points, col_points, panel, half):
    dim, rows = row_points.shape
    col_dev, width = panel.shape
    part = jax.ShapeDtypeStruct((rows // 2, width), F32)
    whole, remote = pl.BlockSpec(memory_space=pltpu.VMEM), pl.BlockSpec(memory_space=pltpu.HBM)
    return pl.pallas_call(
        functools.partial(sketch_body, 2.0 / dim),
        in_specs=[pl.BlockSpec(memory_space=pltpu.SMEM), remote, remote, remote],
        out_specs=[whole, whole],
        out_shape=[part, part],
        scratch_shapes=[
            pltpu.VMEM((dim, rows), BF16),
            pltpu.VMEM((dim, col_dev), BF16),
            pltpu.VMEM((col_dev, width), BF16),
            pltpu.VMEM((rows, col_dev), BF16),
            pltpu.VMEM((rows, width), F32),
            pltpu.SemaphoreType.DMA,
            pltpu.SemaphoreType.DMA,
            pltpu.SemaphoreType.DMA,
        ],
        compiler_params=pltpu.CompilerParams(vmem_limit_bytes=VMEM_BYTES),
        name="sketch",
    )(half, *[pltpu.with_memory_space_constraint(a, pltpu.HBM) for a in (row_points, col_points, panel)])


def inverse_factor(gram, after_step):
    n = gram.shape[0]
    tiles = n // 8
    left = [gram[8 * t : 8 * t + 8, :] for t in range(tiles)]
    lane = lax.broadcasted_iota(jnp.int32, (8, n), 1)
    sub = lax.broadcasted_iota(jnp.int32, (8, n), 0)
    right = [jnp.where(lane == sub + 8 * t, 1.0, 0.0) for t in range(tiles)]
    inverse = []

    def row(tile, k):
        return jnp.broadcast_to(tile[k : k + 1, :], (8, n))

    def column(tile, k):
        return jnp.broadcast_to(tile[:, k : k + 1], (8, n))

    def weighted(weights, rows):
        pairs = [w * r for w, r in zip(weights, rows)]
        while len(pairs) > 1:
            pairs = [a + b for a, b in zip(pairs[::2], pairs[1::2])]
        return pairs[0]

    def terms(x):
        high = x.astype(BF16).astype(F32)
        middle = (x - high).astype(BF16).astype(F32)
        return high, middle, x - high - middle

    for b in range(tiles):
        upper, lower = left[b], right[b]
        block = [column(upper, 8 * b + k) for k in range(8)]
        root, below = [], []
        for k in range(8):
            under = {j: row(block[k], j) for j in range(k + 1, 8)}
            root.append(lax.rsqrt(row(block[k], k)))
            square = root[k] * root[k]
            step = jnp.where(sub > k, block[k] * root[k], 0.0)
            for j in range(k + 1, 8):
                block[j] = block[j] - (block[k] * under[j]) * square
            below.append({j: under[j] * root[k] for j in under})
            upper_row, lower_row = row(upper, k) * root[k], row(lower, k) * root[k]
            upper, lower = upper - step * upper_row, lower - step * lower_row
        scales = root[0]
        for k in range(1, 8):
            scales = jnp.where(sub == k, root[k], scales)
        upper, lower = upper * scales, lower * scales
        inverse.append(lower)
        after_step((b + 1) / tiles)
        if b + 1 == tiles:
            break
        t = b + 1
        entry = [column(left[t], 8 * b + k) for k in range(8)]
        for k in range(8):
            entry[k] = entry[k] * root[k]
            for j in range(k + 1, 8):
                entry[j] = entry[j] - entry[k] * below[k][j]
        left[t] = left[t] - weighted(entry, [row(upper, k) for k in range(8)])
        right[t] = right[t] - weighted(entry, [row(lower, k) for k in range(8)])
        if t + 1 < tiles:
            high, middle, low = terms(upper)
            right_high, right_middle, right_low = terms(lower)
            weights = jnp.concatenate([high, high, middle, high, low, middle], axis=0)
            uppers = jnp.concatenate([high, middle, high, low, high, middle], axis=0)
            lowers = jnp.concatenate(
                [right_high, right_middle, right_high, right_low, right_high, right_middle], axis=0
            )
            both_sides = jnp.concatenate([uppers, lowers], axis=1).astype(BF16)
            update = contract(weights.astype(BF16), both_sides, 0, 0)
            for t in range(b + 2, tiles):
                left[t] = left[t] - update[8 * t : 8 * t + 8, :n]
                right[t] = right[t] - update[8 * t : 8 * t + 8, n:]
    return inverse


def finish_body(
    scale, norm, stored, rank_ref, sketch_ref, row_ref, col_ref, left_basis_ref, out_ref, inverse_ref, left_ref, tile_ref
):
    blocks, _, rows = row_ref.shape
    total, col_dev = left_ref.shape[0], col_ref.shape[1]
    chunk = tile_ref.shape[1] if not stored else chunk_width(col_dev) // 2
    sketch = sketch_ref[...]
    gram = contract(sketch, sketch, 0, 0, EXACT)
    for k in range(blocks):
        left_ref[k * rows : (k + 1) * rows, :] = widened(row_ref[k], scale, 2.0 * scale, True).T
    work = list(range(0, col_dev, chunk)) if stored else []
    done = 0

    def tiles_until(share):
        nonlocal done
        upto = int(len(work) * share)
        for c in work[done:upto]:
            right = widened(col_ref[:, c : c + chunk], scale, 1.0, False)
            tile_ref[:, c : c + chunk] = exponent(left_ref[...], right)
        done = upto

    for t, tile in enumerate(inverse_factor(gram, tiles_until)):
        inverse_ref[8 * t : 8 * t + 8, :] = tile
    left_basis_ref[...] = contract(sketch_ref[:rows, :], inverse_ref[...], 1, 1, EXACT) * norm
    count = out_ref.shape[0]
    mine = inverse_ref[pl.ds(pl.multiple_of(rank_ref[0] * count, count), count), :]
    ranks = contract(mine, sketch_ref[...], 1, 1, EXACT).astype(BF16)
    if stored:
        for c in range(0, col_dev, 2 * chunk):
            at = slice(c, c + 2 * chunk)
            out_ref[:, at] = contract(ranks, tile_ref[:, at], 1, 0).astype(BF16)
    else:

        @pl.loop(0, col_dev // chunk)
        def _(k):
            at = pl.ds(pl.multiple_of(k * chunk, chunk), chunk)
            tile_ref[...] = exponent(left_ref[...], widened(col_ref[:, at], scale, 1.0, False))
            out_ref[:, at] = contract(ranks, tile_ref[...], 1, 0).astype(BF16)


def finish(index, sketch, row_blocks, col_points):
    total, width = sketch.shape
    blocks, dim, rows = row_blocks.shape
    col_dev = col_points.shape[1]
    stored = total * col_dev * 2 <= TILE_BYTES
    count = width // blocks
    whole = pl.BlockSpec(memory_space=pltpu.VMEM)
    return pl.pallas_call(
        functools.partial(finish_body, 2.0 / dim, math.sqrt(total), stored),
        in_specs=[pl.BlockSpec(memory_space=pltpu.SMEM), whole, whole, whole],
        out_specs=[whole, whole],
        out_shape=[jax.ShapeDtypeStruct((rows, width), F32), jax.ShapeDtypeStruct((count, col_dev), BF16)],
        scratch_shapes=[
            pltpu.VMEM((width, width), F32),
            pltpu.VMEM((total, dim + 16), BF16),
            pltpu.VMEM((total, col_dev if stored else math.gcd(col_dev, 512)), BF16),
        ],
        compiler_params=pltpu.CompilerParams(vmem_limit_bytes=VMEM_BYTES),
        name="finish",
    )(index, sketch, row_blocks, col_points)


def swapped(value, row_bit, col_bit):
    rows, cols = lax.axis_size("row"), lax.axis_size("col")
    pairs = [(r * cols + c, (r ^ row_bit) * cols + (c ^ col_bit)) for r in range(rows) for c in range(cols)]
    return lax.ppermute(value, ("row", "col"), pairs)


def bits_down(size):
    return [1 << k for k in reversed(range(size.bit_length() - 1))]


def per_device(row_points, col_points, random_panel):
    row_count, col_count = lax.axis_size("row"), lax.axis_size("col")
    half = lax.axis_index("col") % 2
    row_bits, col_bits = bits_down(row_count), bits_down(col_count)
    keep, send = sketch_halves(row_points, col_points, random_panel, half.reshape(1))

    def both(blocks, moved):
        return jnp.concatenate([blocks, moved], axis=0)

    first = half == 0

    def ordered(mine, other, axis=0):
        return jnp.concatenate([jnp.where(first, mine, other), jnp.where(first, other, mine)], axis=axis)

    part = keep + swapped(send, 0, 1)
    for bit in reversed(col_bits[:-1]):
        part = part + swapped(part, 0, bit)

    bit, *more_bits = row_bits
    dim, rows = row_points.shape
    points = lax.dynamic_slice_in_dim(row_points, half * (rows // 2), rows // 2, 1).astype(F32)
    message, part = lax.optimization_barrier((both(part, points), part))
    cross, far, near = swapped(message, bit, 1), swapped(message, bit, 0), swapped(part, 0, 1)
    split = part.shape[0]
    sketch = both(ordered(part, near), ordered(far[:split], cross[:split]))
    moved = ordered(far[split:], cross[split:], 1).astype(BF16)
    row_blocks = jnp.stack([row_points, moved])
    for bit in more_bits:
        sketch, row_blocks = [both(a, swapped(a, bit, 0)) for a in (sketch, row_blocks)]
    return finish(lax.axis_index("row").reshape(1), sketch, row_blocks, col_points)


def solution(mesh):
    placed = (P(None, "row"), P(None, "col"), P("col", None))
    return jax.shard_map(
        per_device,
        mesh=mesh,
        in_specs=placed,
        out_specs=(P("row", None), P("row", "col")),
        check_vma=False,
    )
```

```python
import functools
import math

import jax
import jax.numpy as jnp
from jax import lax
from jax.experimental import pallas as pl
from jax.experimental.pallas import tpu as pltpu
from jax.sharding import PartitionSpec as P

F32 = jnp.float32
BF16 = jnp.bfloat16
EXACT = lax.Precision.HIGHEST
VMEM_BYTES = 40 << 20
CHUNK = 512


def contract(a, b, a_dim, b_dim, precision=None):
    dims = (((a_dim,), (b_dim,)), ((), ()))
    return lax.dot_general(a, b, dims, precision=precision, preferred_element_type=F32)


def widened(points, scale, factor, first):
    wide = points.astype(F32)
    terms_sum = -scale * jnp.sum(wide * wide, axis=0, keepdims=True)
    place = lax.broadcasted_iota(jnp.int32, (16, points.shape[1]), 0)
    terms_at, ones_at = (0, 3) if first else (3, 0)
    extra = jnp.where((place >= ones_at) & (place < ones_at + 3), 1.0, 0.0)
    for k in range(3):
        term = terms_sum.astype(BF16).astype(F32)
        extra = jnp.where(place == terms_at + k, term, extra)
        terms_sum = terms_sum - term
    return jnp.concatenate([(wide * factor).astype(BF16), extra.astype(BF16)], axis=0)


def exponent(left, right):
    return jnp.exp(contract(left, right, 1, 0)).astype(BF16)


def chunk_width(col_dev):
    return math.gcd(col_dev, 1024)


def sketch_body(
    scale, half_ref, row_hbm, col_hbm, panel_hbm, keep_ref, send_ref,
    row_ref, col_ref, panel_ref, tile_ref, total_ref, row_sem, col_sem, panel_sem,
):
    row_copy = pltpu.make_async_copy(row_hbm, row_ref, row_sem)
    col_copy = pltpu.make_async_copy(col_hbm, col_ref, col_sem)
    panel_copy = pltpu.make_async_copy(panel_hbm, panel_ref, panel_sem)
    row_copy.start()
    col_copy.start()
    panel_copy.start()
    chunk = chunk_width(col_ref.shape[1])
    row_copy.wait()
    left = widened(row_ref[...], scale, 2.0 * scale, True).T
    col_copy.wait()
    for c in range(0, col_ref.shape[1], chunk):
        right = widened(col_ref[:, c : c + chunk], scale, 1.0, False)
        tile_ref[:, c : c + chunk] = exponent(left, right)
    panel_copy.wait()
    total_ref[...] = contract(tile_ref[...], panel_ref[...], 1, 0)
    half, rows = half_ref[0], keep_ref.shape[0]
    keep_ref[...] = total_ref[pl.ds(pl.multiple_of(half * rows, rows), rows), :]
    send_ref[...] = total_ref[pl.ds(pl.multiple_of((1 - half) * rows, rows), rows), :]


def sketch_halves(row_points, col_points, panel, half):
    dim, rows = row_points.shape
    col_dev, width = panel.shape
    part = jax.ShapeDtypeStruct((rows // 2, width), F32)
    whole, remote = pl.BlockSpec(memory_space=pltpu.VMEM), pl.BlockSpec(memory_space=pltpu.HBM)
    return pl.pallas_call(
        functools.partial(sketch_body, 2.0 / dim),
        in_specs=[pl.BlockSpec(memory_space=pltpu.SMEM), remote, remote, remote],
        out_specs=[whole, whole],
        out_shape=[part, part],
        scratch_shapes=[
            pltpu.VMEM((dim, rows), BF16),
            pltpu.VMEM((dim, col_dev), BF16),
            pltpu.VMEM((col_dev, width), BF16),
            pltpu.VMEM((rows, col_dev), BF16),
            pltpu.VMEM((rows, width), F32),
            pltpu.SemaphoreType.DMA,
            pltpu.SemaphoreType.DMA,
            pltpu.SemaphoreType.DMA,
        ],
        compiler_params=pltpu.CompilerParams(vmem_limit_bytes=VMEM_BYTES),
        name="sketch",
    )(half, *[pltpu.with_memory_space_constraint(a, pltpu.HBM) for a in (row_points, col_points, panel)])


def inverse_factor(gram, after_step):
    n = gram.shape[0]
    tiles = n // 8
    left = [gram[8 * t : 8 * t + 8, :] for t in range(tiles)]
    lane = lax.broadcasted_iota(jnp.int32, (8, n), 1)
    sub = lax.broadcasted_iota(jnp.int32, (8, n), 0)
    right = [jnp.where(lane == sub + 8 * t, 1.0, 0.0) for t in range(tiles)]
    inverse = []

    def row(tile, k):
        return jnp.broadcast_to(tile[k : k + 1, :], (8, n))

    def column(tile, k):
        return jnp.broadcast_to(tile[:, k : k + 1], (8, n))

    def weighted(weights, rows):
        pairs = [w * r for w, r in zip(weights, rows)]
        while len(pairs) > 1:
            pairs = [a + b for a, b in zip(pairs[::2], pairs[1::2])]
        return pairs[0]

    for b in range(tiles):
        upper, lower = left[b], right[b]
        block = [column(upper, 8 * b + k) for k in range(8)]
        root, below = [], []
        for k in range(8):
            root.append(lax.rsqrt(row(block[k], k)))
            step = jnp.where(sub > k, block[k] * root[k], 0.0)
            below.append({j: row(step, j) for j in range(k + 1, 8)})
            for j in range(k + 1, 8):
                block[j] = block[j] - step * below[k][j]
            upper_row, lower_row = row(upper, k) * root[k], row(lower, k) * root[k]
            upper, lower = upper - step * upper_row, lower - step * lower_row
        scales = root[0]
        for k in range(1, 8):
            scales = jnp.where(sub == k, root[k], scales)
        upper, lower = upper * scales, lower * scales
        inverse.append(lower)
        after_step((b + 1) / tiles)
        upper_rows = [row(upper, k) for k in range(8)]
        lower_rows = [row(lower, k) for k in range(8)]
        for t in range(b + 1, tiles):
            entry = [column(left[t], 8 * b + k) for k in range(8)]
            for k in range(8):
                entry[k] = entry[k] * root[k]
                for j in range(k + 1, 8):
                    entry[j] = entry[j] - entry[k] * below[k][j]
            left[t] = left[t] - weighted(entry, upper_rows)
            right[t] = right[t] - weighted(entry, lower_rows)
    return inverse


def bf16_terms(x):
    high = x.astype(BF16)
    rest = x - high.astype(F32)
    middle = rest.astype(BF16)
    return high, middle, (rest - middle.astype(F32)).astype(BF16)


def finish_body(
    scale, norm, chunk, rank_ref, sketch_ref, row_ref, col_ref, left_basis_ref, keep_ref, send_ref,
    inverse_ref, left_ref, sketch_t_ref, *term_refs,
):
    blocks, _, rows = row_ref.shape
    sketch = sketch_ref[...]
    width = sketch.shape[1]
    gram = contract(sketch, sketch, 0, 0, EXACT)
    high, middle, _ = bf16_terms(sketch)
    sketch_t_ref[:width, :] = high.T
    sketch_t_ref[width:, :] = middle.T
    for k in range(blocks):
        left_ref[k * rows : (k + 1) * rows, :] = widened(row_ref[k], scale, 2.0 * scale, True).T
    starts = list(range(0, col_ref.shape[1], chunk))
    pending, done = [], 0

    def finish_pending():
        for c, tile in pending:
            product = contract(sketch_t_ref[...], tile, 1, 0)
            for ref, term in zip(term_refs, bf16_terms(product[:width] + product[width:])):
                ref[:, c : c + chunk] = term
        pending.clear()

    def projected_until(share):
        nonlocal done
        upto = int(len(starts) * share)
        for c in starts[done:upto]:
            finish_pending()
            tile = exponent(left_ref[...], widened(col_ref[:, c : c + chunk], scale, 1.0, False))
            pending.append((c, tile))
        done = upto
        if share == 1.0:
            finish_pending()

    for t, tile in enumerate(inverse_factor(gram, projected_until)):
        inverse_ref[8 * t : 8 * t + 8, :] = tile
    left_basis_ref[...] = contract(sketch_ref[:rows, :], inverse_ref[...], 1, 1, EXACT) * norm
    count = keep_ref.shape[0]
    mine = [inverse_ref[pl.ds(pl.multiple_of(rank_ref[k] * count, count), count), :] for k in range(2)]
    terms = bf16_terms(jnp.concatenate(mine, axis=0))
    for c in range(0, col_ref.shape[1], 2 * chunk):
        at = slice(c, c + 2 * chunk)
        total = None
        for k, ref in enumerate(term_refs):
            stack = jnp.concatenate(terms[: 3 - k], axis=0)
            product = contract(stack, ref[:, at], 1, 0)
            for j in range(3 - k):
                piece = product[2 * count * j : 2 * count * (j + 1)]
                total = piece if total is None else total + piece
        keep_ref[:, at] = total[:count].astype(BF16)
        send_ref[:, at] = total[count:].astype(BF16)


def finish(index, sketch, row_blocks, col_points):
    total, width = sketch.shape
    blocks, dim, rows = row_blocks.shape
    col_dev = col_points.shape[1]
    part = jax.ShapeDtypeStruct((width // blocks, col_dev), BF16)
    whole = pl.BlockSpec(memory_space=pltpu.VMEM)
    return pl.pallas_call(
        functools.partial(finish_body, 2.0 / dim, math.sqrt(total), math.gcd(col_dev, CHUNK)),
        in_specs=[pl.BlockSpec(memory_space=pltpu.SMEM), whole, whole, whole],
        out_specs=[whole, whole, whole],
        out_shape=[jax.ShapeDtypeStruct((rows, width), F32), part, part],
        scratch_shapes=[
            pltpu.VMEM((width, width), F32),
            pltpu.VMEM((total, dim + 16), BF16),
            pltpu.VMEM((2 * width, total), BF16),
            *[pltpu.VMEM((width, col_dev), BF16)] * 3,
        ],
        compiler_params=pltpu.CompilerParams(vmem_limit_bytes=VMEM_BYTES),
        name="finish",
    )(index, sketch, row_blocks, col_points)


def place_body(at_ref, part_ref, *refs):
    out_hbm, sem = refs[-2:]
    width = part_ref.shape[1]
    at = pl.ds(pl.multiple_of(at_ref[0] * width, width), width)
    copy = pltpu.make_async_copy(part_ref, out_hbm.at[:, at], sem)
    copy.start()
    copy.wait()


def placed(part, at, out=None):
    count, width = part.shape
    remote = pl.BlockSpec(memory_space=pltpu.HBM)
    specs = [pl.BlockSpec(memory_space=pltpu.SMEM), pl.BlockSpec(memory_space=pltpu.VMEM)]
    operands = [at.reshape(1), part]
    if out is not None:
        specs.append(remote)
        operands.append(out)
    return pl.pallas_call(
        place_body,
        in_specs=specs,
        out_specs=remote,
        out_shape=jax.ShapeDtypeStruct((count, 2 * width), part.dtype),
        scratch_shapes=[pltpu.SemaphoreType.DMA],
        input_output_aliases={} if out is None else {2: 0},
        compiler_params=pltpu.CompilerParams(vmem_limit_bytes=VMEM_BYTES),
        cost_estimate=pl.CostEstimate(flops=0, bytes_accessed=4 * count * width, transcendentals=0),
        name="placed",
    )(*operands)


def swapped(value, row_bit, col_bit):
    rows, cols = lax.axis_size("row"), lax.axis_size("col")
    pairs = [(r * cols + c, (r ^ row_bit) * cols + (c ^ col_bit)) for r in range(rows) for c in range(cols)]
    return lax.ppermute(value, ("row", "col"), pairs)


def bits_up(size):
    return [1 << k for k in range(size.bit_length() - 1)]


def per_device(row_points, col_points, random_panel):
    core_bit, *y_bits = bits_up(lax.axis_size("row"))
    x_bit, *z_bits = bits_up(lax.axis_size("col"))
    half = lax.axis_index("col") % 2
    keep, send = sketch_halves(row_points, col_points, random_panel, half.reshape(1))

    def both(a, b, axis=0):
        return jnp.concatenate([a, b], axis=axis)

    def ordered(mine, other, axis=0):
        return both(jnp.where(half == 0, mine, other), jnp.where(half == 0, other, mine), axis)

    part = keep + swapped(send, 0, x_bit)
    for bit in z_bits:
        part = part + swapped(part, 0, bit)

    dim, rows = row_points.shape
    points = lax.dynamic_slice_in_dim(row_points, half * (rows // 2), rows // 2, 1).astype(F32)
    message = both(part, points)
    y_bit = y_bits[-1]
    near = swapped(part, core_bit, x_bit)
    cross, far = swapped(message, y_bit, x_bit), swapped(message, core_bit | y_bit, 0)
    split = part.shape[0]
    held = jnp.concatenate([part, near, far[:split], cross[:split]])
    held_points = jnp.stack([row_points, both(far[split:], cross[split:], 1).astype(BF16)])
    there, there_points = swapped(held, core_bit, 0), swapped(held_points, core_bit, 0)
    part, near, far, cross = held.reshape(4, split, -1)
    part_there, near_there, far_there, cross_there = there.reshape(4, split, -1)
    (points, far_points, cross_points), (points_there, far_points_there, cross_points_there) = [
        (a[0], a[1][:, : rows // 2], a[1][:, rows // 2 :]) for a in (held_points, there_points)
    ]
    sketch = [ordered(part, near_there), ordered(part_there, near)]
    row_blocks = [points, points_there]
    sketch += [ordered(far, cross_there), ordered(far_there, cross)]
    row_blocks += [ordered(far_points, cross_points_there, 1), ordered(far_points_there, cross_points, 1)]
    sketch, row_blocks = jnp.concatenate(sketch), jnp.stack(row_blocks)
    for bit in y_bits[:-1]:
        sketch, row_blocks = [both(a, swapped(a, bit, 0)) for a in (sketch, row_blocks)]

    row_at = lax.axis_index("row")
    core = row_at % 2
    width = col_points.shape[1] // 2
    columns = lax.dynamic_slice_in_dim(col_points, core * width, width, 1)
    left_basis, kept, sent = finish(jnp.stack([row_at, row_at ^ core_bit]), sketch, row_blocks, columns)
    received = swapped(sent, core_bit, 0)
    return left_basis, placed(received, 1 - core, placed(kept, core))


def solution(mesh):
    placed = (P(None, "row"), P(None, "col"), P("col", None))
    return jax.shard_map(
        per_device,
        mesh=mesh,
        in_specs=placed,
        out_specs=(P("row", None), P("row", "col")),
        check_vma=False,
    )
```

```python
import functools
import math

import jax
import jax.numpy as jnp
from jax import lax
from jax.experimental import pallas as pl
from jax.experimental.pallas import tpu as pltpu
from jax.sharding import PartitionSpec as P

F32 = jnp.float32
BF16 = jnp.bfloat16
EXACT = lax.Precision.HIGHEST
VMEM_BYTES = 40 << 20
SKETCH_VMEM_BYTES = 16 << 20
CHUNK = 512


def contract(a, b, a_dim, b_dim, precision=None):
    dims = (((a_dim,), (b_dim,)), ((), ()))
    return lax.dot_general(a, b, dims, precision=precision, preferred_element_type=F32)


def widened(points, scale, factor, first):
    wide = points.astype(F32)
    terms_sum = -scale * jnp.sum(wide * wide, axis=0, keepdims=True)
    place = lax.broadcasted_iota(jnp.int32, (16, points.shape[1]), 0)
    terms_at, ones_at = (0, 3) if first else (3, 0)
    extra = jnp.where((place >= ones_at) & (place < ones_at + 3), 1.0, 0.0)
    for k in range(3):
        term = terms_sum.astype(BF16).astype(F32)
        extra = jnp.where(place == terms_at + k, term, extra)
        terms_sum = terms_sum - term
    return jnp.concatenate([(wide * factor).astype(BF16), extra.astype(BF16)], axis=0)


def exponent(left, right):
    return jnp.exp(contract(left, right, 1, 0)).astype(BF16)


def chunk_width(col_dev):
    return math.gcd(col_dev, 1024)


def half_left(row_points, scale, half, left_ref):
    left_ref[...] = widened(row_points, scale, 2.0 * scale, True).T
    rows = left_ref.shape[0] // 2
    return left_ref[pl.ds(pl.multiple_of(half * rows, rows), rows), :]


def sketch_send_body(
    scale, half_ref, row_hbm, col_hbm, panel_hbm, send_ref, col_ref, panel_ref,
    row_ref, left_ref, tile_ref, row_sem, col_sem, panel_sem,
):
    row_copy = pltpu.make_async_copy(row_hbm, row_ref, row_sem)
    col_copy = pltpu.make_async_copy(col_hbm, col_ref, col_sem)
    panel_copy = pltpu.make_async_copy(panel_hbm, panel_ref, panel_sem)
    row_copy.start()
    col_copy.start()
    panel_copy.start()
    chunk = chunk_width(col_ref.shape[1])
    row_copy.wait()
    left = half_left(row_ref[...], scale, 1 - half_ref[0], left_ref)
    col_copy.wait()
    for c in range(0, col_ref.shape[1], chunk):
        right = widened(col_ref[:, c : c + chunk], scale, 1.0, False)
        tile_ref[:, c : c + chunk] = exponent(left, right)
    panel_copy.wait()
    send_ref[...] = contract(tile_ref[...], panel_ref[...], 1, 0)


def sketch_keep_body(scale, half_ref, row_ref, col_ref, panel_ref, keep_ref, left_ref):
    left = half_left(row_ref[...], scale, half_ref[0], left_ref)
    chunk = chunk_width(col_ref.shape[1])
    total = jnp.zeros(keep_ref.shape, F32)
    for c in range(0, col_ref.shape[1], chunk):
        tile = exponent(left, widened(col_ref[:, c : c + chunk], scale, 1.0, False))
        total = total + contract(tile, panel_ref[c : c + chunk, :], 1, 0)
    keep_ref[...] = total


def sketch_halves(row_points, col_points, panel, half):
    dim, rows = row_points.shape
    col_dev, width = panel.shape
    part = jax.ShapeDtypeStruct((rows // 2, width), F32)
    whole, remote = pl.BlockSpec(memory_space=pltpu.VMEM), pl.BlockSpec(memory_space=pltpu.HBM)
    scalar = pl.BlockSpec(memory_space=pltpu.SMEM)
    send, col_near, panel_near = pl.pallas_call(
        functools.partial(sketch_send_body, 2.0 / dim),
        in_specs=[scalar, remote, remote, remote],
        out_specs=[whole, whole, whole],
        out_shape=[
            part,
            jax.ShapeDtypeStruct((dim, col_dev), BF16),
            jax.ShapeDtypeStruct((col_dev, width), BF16),
        ],
        scratch_shapes=[
            pltpu.VMEM((dim, rows), BF16),
            pltpu.VMEM((rows, dim + 16), BF16),
            pltpu.VMEM((rows // 2, col_dev), BF16),
            pltpu.SemaphoreType.DMA,
            pltpu.SemaphoreType.DMA,
            pltpu.SemaphoreType.DMA,
        ],
        compiler_params=pltpu.CompilerParams(vmem_limit_bytes=SKETCH_VMEM_BYTES),
        name="sketch_send",
    )(half, *[pltpu.with_memory_space_constraint(a, pltpu.HBM) for a in (row_points, col_points, panel)])
    keep = pl.pallas_call(
        functools.partial(sketch_keep_body, 2.0 / dim),
        in_specs=[scalar, whole, whole, whole],
        out_specs=whole,
        out_shape=part,
        scratch_shapes=[pltpu.VMEM((rows, dim + 16), BF16)],
        compiler_params=pltpu.CompilerParams(vmem_limit_bytes=SKETCH_VMEM_BYTES),
        cost_estimate=pl.CostEstimate(
            flops=rows * col_dev * (dim + 16 + width),
            bytes_accessed=2 * col_dev * (dim + 16 + width),
            transcendentals=rows // 2 * col_dev,
        ),
        name="sketch_keep",
    )(half, row_points, col_near, panel_near)
    return keep, send


def inverse_factor(gram, after_step):
    n = gram.shape[0]
    tiles = n // 8
    left = [gram[8 * t : 8 * t + 8, :] for t in range(tiles)]
    lane = lax.broadcasted_iota(jnp.int32, (8, n), 1)
    sub = lax.broadcasted_iota(jnp.int32, (8, n), 0)
    right = [jnp.where(lane == sub + 8 * t, 1.0, 0.0) for t in range(tiles)]
    inverse = []

    def row(tile, k):
        return jnp.broadcast_to(tile[k : k + 1, :], (8, n))

    def column(tile, k):
        return jnp.broadcast_to(tile[:, k : k + 1], (8, n))

    def weighted(weights, rows):
        pairs = [w * r for w, r in zip(weights, rows)]
        while len(pairs) > 1:
            pairs = [a + b for a, b in zip(pairs[::2], pairs[1::2])]
        return pairs[0]

    for b in range(tiles):
        upper, lower = left[b], right[b]
        block = [column(upper, 8 * b + k) for k in range(8)]
        root, below = [], []
        for k in range(8):
            root.append(lax.rsqrt(row(block[k], k)))
            step = jnp.where(sub > k, block[k] * root[k], 0.0)
            below.append({j: row(step, j) for j in range(k + 1, 8)})
            for j in range(k + 1, 8):
                block[j] = block[j] - step * below[k][j]
            upper_row, lower_row = row(upper, k) * root[k], row(lower, k) * root[k]
            upper, lower = upper - step * upper_row, lower - step * lower_row
        scales = root[0]
        for k in range(1, 8):
            scales = jnp.where(sub == k, root[k], scales)
        upper, lower = upper * scales, lower * scales
        inverse.append(lower)
        after_step((b + 1) / tiles)
        upper_rows = [row(upper, k) for k in range(8)]
        lower_rows = [row(lower, k) for k in range(8)]
        for t in range(b + 1, tiles):
            entry = [column(left[t], 8 * b + k) for k in range(8)]
            for k in range(8):
                entry[k] = entry[k] * root[k]
                for j in range(k + 1, 8):
                    entry[j] = entry[j] - entry[k] * below[k][j]
            left[t] = left[t] - weighted(entry, upper_rows)
            right[t] = right[t] - weighted(entry, lower_rows)
    return inverse


def bf16_terms(x):
    high = x.astype(BF16)
    rest = x - high.astype(F32)
    middle = rest.astype(BF16)
    return high, middle, (rest - middle.astype(F32)).astype(BF16)


def finish_body(
    scale, norm, chunk, rank_ref, sketch_ref, row_ref, col_ref, left_basis_ref, keep_ref, send_ref,
    inverse_ref, left_ref, sketch_t_ref, *term_refs,
):
    blocks, _, rows = row_ref.shape
    sketch = sketch_ref[...]
    width = sketch.shape[1]
    high, middle, low = bf16_terms(sketch)
    for k, term in enumerate((high, middle, low)):
        sketch_t_ref[k * width : (k + 1) * width, :] = term.T
    with_high = contract(sketch_t_ref[...], high, 1, 0)
    mixed = with_high[width : 2 * width] + with_high[2 * width :]
    middles = contract(sketch_t_ref[width : 2 * width, :], middle, 1, 0)
    gram = with_high[:width] + ((mixed + mixed.T) + middles)
    for k in range(blocks):
        left_ref[k * rows : (k + 1) * rows, :] = widened(row_ref[k], scale, 2.0 * scale, True).T
    starts = list(range(0, col_ref.shape[1], chunk))
    pending, done = [], 0

    def finish_pending():
        for c, tile in pending:
            product = contract(sketch_t_ref[: 2 * width, :], tile, 1, 0)
            for ref, term in zip(term_refs, bf16_terms(product[:width] + product[width:])):
                ref[:, c : c + chunk] = term
        pending.clear()

    def projected_until(share):
        nonlocal done
        upto = int(len(starts) * share)
        for c in starts[done:upto]:
            finish_pending()
            tile = exponent(left_ref[...], widened(col_ref[:, c : c + chunk], scale, 1.0, False))
            pending.append((c, tile))
        done = upto
        if share == 1.0:
            finish_pending()

    for t, tile in enumerate(inverse_factor(gram, projected_until)):
        inverse_ref[8 * t : 8 * t + 8, :] = tile
    left_basis_ref[...] = contract(sketch_ref[:rows, :], inverse_ref[...], 1, 1, EXACT) * norm
    count = keep_ref.shape[0]
    mine = [inverse_ref[pl.ds(pl.multiple_of(rank_ref[k] * count, count), count), :] for k in range(2)]
    terms = bf16_terms(jnp.concatenate(mine, axis=0))
    for c in range(0, col_ref.shape[1], 2 * chunk):
        at = slice(c, c + 2 * chunk)
        total = None
        for k, ref in enumerate(term_refs):
            stack = jnp.concatenate(terms[: 3 - k], axis=0)
            product = contract(stack, ref[:, at], 1, 0)
            for j in range(3 - k):
                piece = product[2 * count * j : 2 * count * (j + 1)]
                total = piece if total is None else total + piece
        keep_ref[:, at] = total[:count].astype(BF16)
        send_ref[:, at] = total[count:].astype(BF16)


def finish(index, sketch, row_blocks, col_points):
    total, width = sketch.shape
    blocks, dim, rows = row_blocks.shape
    col_dev = col_points.shape[1]
    part = jax.ShapeDtypeStruct((width // blocks, col_dev), BF16)
    whole = pl.BlockSpec(memory_space=pltpu.VMEM)
    return pl.pallas_call(
        functools.partial(finish_body, 2.0 / dim, math.sqrt(total), math.gcd(col_dev, CHUNK)),
        in_specs=[pl.BlockSpec(memory_space=pltpu.SMEM), whole, whole, whole],
        out_specs=[whole, whole, whole],
        out_shape=[jax.ShapeDtypeStruct((rows, width), F32), part, part],
        scratch_shapes=[
            pltpu.VMEM((width, width), F32),
            pltpu.VMEM((total, dim + 16), BF16),
            pltpu.VMEM((3 * width, total), BF16),
            *[pltpu.VMEM((width, col_dev), BF16)] * 3,
        ],
        compiler_params=pltpu.CompilerParams(vmem_limit_bytes=VMEM_BYTES),
        name="finish",
    )(index, sketch, row_blocks, col_points)


def place_body(at_ref, part_ref, *refs):
    out_hbm, sem = refs[-2:]
    width = part_ref.shape[1]
    at = pl.ds(pl.multiple_of(at_ref[0] * width, width), width)
    copy = pltpu.make_async_copy(part_ref, out_hbm.at[:, at], sem)
    copy.start()
    copy.wait()


def placed(part, at, out=None):
    count, width = part.shape
    remote = pl.BlockSpec(memory_space=pltpu.HBM)
    specs = [pl.BlockSpec(memory_space=pltpu.SMEM), pl.BlockSpec(memory_space=pltpu.VMEM)]
    operands = [at.reshape(1), part]
    if out is not None:
        specs.append(remote)
        operands.append(out)
    return pl.pallas_call(
        place_body,
        in_specs=specs,
        out_specs=remote,
        out_shape=jax.ShapeDtypeStruct((count, 2 * width), part.dtype),
        scratch_shapes=[pltpu.SemaphoreType.DMA],
        input_output_aliases={} if out is None else {2: 0},
        compiler_params=pltpu.CompilerParams(vmem_limit_bytes=VMEM_BYTES),
        cost_estimate=pl.CostEstimate(flops=0, bytes_accessed=4 * count * width, transcendentals=0),
        name="placed",
    )(*operands)


def swapped(value, row_bit, col_bit):
    rows, cols = lax.axis_size("row"), lax.axis_size("col")
    pairs = [(r * cols + c, (r ^ row_bit) * cols + (c ^ col_bit)) for r in range(rows) for c in range(cols)]
    return lax.ppermute(value, ("row", "col"), pairs)


def bits_up(size):
    return [1 << k for k in range(size.bit_length() - 1)]


def per_device(row_points, col_points, random_panel):
    core_bit, *y_bits = bits_up(lax.axis_size("row"))
    x_bit, *z_bits = bits_up(lax.axis_size("col"))
    half = lax.axis_index("col") % 2
    keep, send = sketch_halves(row_points, col_points, random_panel, half.reshape(1))

    def both(a, b, axis=0):
        return jnp.concatenate([a, b], axis=axis)

    def ordered(mine, other, axis=0):
        return both(jnp.where(half == 0, mine, other), jnp.where(half == 0, other, mine), axis)

    part = keep + swapped(send, 0, x_bit)
    part, col_points = lax.optimization_barrier((part, col_points))
    for bit in z_bits:
        part = part + swapped(part, 0, bit)

    dim, rows = row_points.shape
    points = lax.dynamic_slice_in_dim(row_points, half * (rows // 2), rows // 2, 1).astype(F32)
    message, part = lax.optimization_barrier((both(part, points), part))
    y_bit = y_bits[-1]
    far = swapped(message, core_bit | y_bit, 0)
    cross = swapped(message, y_bit, x_bit)
    near = swapped(part, core_bit, x_bit)
    split = part.shape[0]
    held = jnp.concatenate([part, near, far[:split], cross[:split]])
    held_points = jnp.stack([row_points, both(far[split:], cross[split:], 1).astype(BF16)])
    there, there_points = swapped(held, core_bit, 0), swapped(held_points, core_bit, 0)
    part, near, far, cross = held.reshape(4, split, -1)
    part_there, near_there, far_there, cross_there = there.reshape(4, split, -1)
    (points, far_points, cross_points), (points_there, far_points_there, cross_points_there) = [
        (a[0], a[1][:, : rows // 2], a[1][:, rows // 2 :]) for a in (held_points, there_points)
    ]
    sketch = [ordered(part, near_there), ordered(part_there, near)]
    row_blocks = [points, points_there]
    sketch += [ordered(far, cross_there), ordered(far_there, cross)]
    row_blocks += [ordered(far_points, cross_points_there, 1), ordered(far_points_there, cross_points, 1)]
    sketch, row_blocks = jnp.concatenate(sketch), jnp.stack(row_blocks)
    for bit in y_bits[:-1]:
        sketch, row_blocks = [both(a, swapped(a, bit, 0)) for a in (sketch, row_blocks)]

    row_at = lax.axis_index("row")
    core = row_at % 2
    width = col_points.shape[1] // 2
    columns = lax.dynamic_slice_in_dim(col_points, core * width, width, 1)
    left_basis, kept, sent = finish(jnp.stack([row_at, row_at ^ core_bit]), sketch, row_blocks, columns)
    received = swapped(sent, core_bit, 0)
    return left_basis, placed(received, 1 - core, placed(kept, core))


def solution(mesh):
    placed = (P(None, "row"), P(None, "col"), P("col", None))
    return jax.shard_map(
        per_device,
        mesh=mesh,
        in_specs=placed,
        out_specs=(P("row", None), P("row", "col")),
        check_vma=False,
    )
```

```python
import functools
import math

import jax
import jax.numpy as jnp
from jax import lax
from jax.experimental import pallas as pl
from jax.experimental.pallas import tpu as pltpu
from jax.sharding import PartitionSpec as P

F32 = jnp.float32
BF16 = jnp.bfloat16
EXACT = lax.Precision.HIGHEST
VMEM_BYTES = 40 << 20
SKETCH_VMEM_BYTES = 16 << 20
CHUNK = 512


def contract(a, b, a_dim, b_dim, precision=None):
    dims = (((a_dim,), (b_dim,)), ((), ()))
    return lax.dot_general(a, b, dims, precision=precision, preferred_element_type=F32)


def widened(points, scale, factor, first):
    wide = points.astype(F32)
    terms_sum = -scale * jnp.sum(wide * wide, axis=0, keepdims=True)
    place = lax.broadcasted_iota(jnp.int32, (16, points.shape[1]), 0)
    terms_at, ones_at = (0, 3) if first else (3, 0)
    extra = jnp.where((place >= ones_at) & (place < ones_at + 3), 1.0, 0.0)
    for k in range(3):
        term = terms_sum.astype(BF16).astype(F32)
        extra = jnp.where(place == terms_at + k, term, extra)
        terms_sum = terms_sum - term
    return jnp.concatenate([(wide * factor).astype(BF16), extra.astype(BF16)], axis=0)


def exponent(left, right):
    return jnp.exp(contract(left, right, 1, 0)).astype(BF16)


def chunk_width(col_dev):
    return math.gcd(col_dev, 1024)


def half_left(row_points, scale, half, left_ref):
    left_ref[...] = widened(row_points, scale, 2.0 * scale, True).T
    rows = left_ref.shape[0] // 2
    return left_ref[pl.ds(pl.multiple_of(half * rows, rows), rows), :]


def sketch_send_body(
    scale, half_ref, row_hbm, col_hbm, panel_hbm, send_ref, col_ref, panel_ref,
    row_ref, left_ref, tile_ref, row_sem, col_sem, panel_sem,
):
    row_copy = pltpu.make_async_copy(row_hbm, row_ref, row_sem)
    col_copy = pltpu.make_async_copy(col_hbm, col_ref, col_sem)
    panel_copy = pltpu.make_async_copy(panel_hbm, panel_ref, panel_sem)
    row_copy.start()
    col_copy.start()
    panel_copy.start()
    chunk = chunk_width(col_ref.shape[1])
    row_copy.wait()
    left = half_left(row_ref[...], scale, 1 - half_ref[0], left_ref)
    col_copy.wait()
    for c in range(0, col_ref.shape[1], chunk):
        right = widened(col_ref[:, c : c + chunk], scale, 1.0, False)
        tile_ref[:, c : c + chunk] = exponent(left, right)
    panel_copy.wait()
    send_ref[...] = contract(tile_ref[...], panel_ref[...], 1, 0)


def sketch_keep_body(scale, half_ref, row_ref, col_ref, panel_ref, keep_ref, left_ref):
    left = half_left(row_ref[...], scale, half_ref[0], left_ref)
    chunk = chunk_width(col_ref.shape[1])
    total = jnp.zeros(keep_ref.shape, F32)
    for c in range(0, col_ref.shape[1], chunk):
        tile = exponent(left, widened(col_ref[:, c : c + chunk], scale, 1.0, False))
        total = total + contract(tile, panel_ref[c : c + chunk, :], 1, 0)
    keep_ref[...] = total


def sketch_halves(row_points, col_points, panel, half):
    dim, rows = row_points.shape
    col_dev, width = panel.shape
    part = jax.ShapeDtypeStruct((rows // 2, width), F32)
    whole, remote = pl.BlockSpec(memory_space=pltpu.VMEM), pl.BlockSpec(memory_space=pltpu.HBM)
    scalar = pl.BlockSpec(memory_space=pltpu.SMEM)
    send, col_near, panel_near = pl.pallas_call(
        functools.partial(sketch_send_body, 2.0 / dim),
        in_specs=[scalar, remote, remote, remote],
        out_specs=[whole, whole, whole],
        out_shape=[
            part,
            jax.ShapeDtypeStruct((dim, col_dev), BF16),
            jax.ShapeDtypeStruct((col_dev, width), BF16),
        ],
        scratch_shapes=[
            pltpu.VMEM((dim, rows), BF16),
            pltpu.VMEM((rows, dim + 16), BF16),
            pltpu.VMEM((rows // 2, col_dev), BF16),
            pltpu.SemaphoreType.DMA,
            pltpu.SemaphoreType.DMA,
            pltpu.SemaphoreType.DMA,
        ],
        compiler_params=pltpu.CompilerParams(vmem_limit_bytes=SKETCH_VMEM_BYTES),
        name="sketch_send",
    )(half, *[pltpu.with_memory_space_constraint(a, pltpu.HBM) for a in (row_points, col_points, panel)])
    keep = pl.pallas_call(
        functools.partial(sketch_keep_body, 2.0 / dim),
        in_specs=[scalar, whole, whole, whole],
        out_specs=whole,
        out_shape=part,
        scratch_shapes=[pltpu.VMEM((rows, dim + 16), BF16)],
        compiler_params=pltpu.CompilerParams(vmem_limit_bytes=SKETCH_VMEM_BYTES),
        cost_estimate=pl.CostEstimate(
            flops=rows * col_dev * (dim + 16 + width),
            bytes_accessed=2 * col_dev * (dim + 16 + width),
            transcendentals=rows // 2 * col_dev,
        ),
        name="sketch_keep",
    )(half, row_points, col_near, panel_near)
    return keep, send


def inverse_factor(gram, after_step):
    n = gram.shape[0]
    tiles = n // 8
    left = [gram[8 * t : 8 * t + 8, :] for t in range(tiles)]
    lane = lax.broadcasted_iota(jnp.int32, (8, n), 1)
    sub = lax.broadcasted_iota(jnp.int32, (8, n), 0)
    right = [jnp.where(lane == sub + 8 * t, 1.0, 0.0) for t in range(tiles)]
    inverse = []

    def row(tile, k):
        return jnp.broadcast_to(tile[k : k + 1, :], (8, n))

    def column(tile, k):
        return jnp.broadcast_to(tile[:, k : k + 1], (8, n))

    def weighted(weights, rows):
        pairs = [w * r for w, r in zip(weights, rows)]
        while len(pairs) > 1:
            pairs = [a + b for a, b in zip(pairs[::2], pairs[1::2])]
        return pairs[0]

    for b in range(tiles):
        upper, lower = left[b], right[b]
        block = [column(upper, 8 * b + k) for k in range(8)]
        root, below = [], []
        for k in range(8):
            root.append(lax.rsqrt(row(block[k], k)))
            step = jnp.where(sub > k, block[k] * root[k], 0.0)
            below.append({j: row(step, j) for j in range(k + 1, 8)})
            for j in range(k + 1, 8):
                block[j] = block[j] - step * below[k][j]
            upper_row, lower_row = row(upper, k) * root[k], row(lower, k) * root[k]
            upper, lower = upper - step * upper_row, lower - step * lower_row
        scales = root[0]
        for k in range(1, 8):
            scales = jnp.where(sub == k, root[k], scales)
        upper, lower = upper * scales, lower * scales
        inverse.append(lower)
        after_step((b + 1) / tiles)
        upper_rows = [row(upper, k) for k in range(8)]
        lower_rows = [row(lower, k) for k in range(8)]
        for t in range(b + 1, tiles):
            entry = [column(left[t], 8 * b + k) for k in range(8)]
            for k in range(8):
                entry[k] = entry[k] * root[k]
                for j in range(k + 1, 8):
                    entry[j] = entry[j] - entry[k] * below[k][j]
            left[t] = left[t] - weighted(entry, upper_rows)
            right[t] = right[t] - weighted(entry, lower_rows)
    return inverse


def bf16_terms(x):
    high = x.astype(BF16)
    rest = x - high.astype(F32)
    middle = rest.astype(BF16)
    return high, middle, (rest - middle.astype(F32)).astype(BF16)


def finish_body(
    scale, norm, chunk, rank_ref, sketch_ref, row_ref, col_ref, left_basis_ref, keep_ref, send_ref,
    inverse_ref, left_ref, sketch_t_ref, *term_refs,
):
    blocks, _, rows = row_ref.shape
    sketch = sketch_ref[...]
    width = sketch.shape[1]
    high, middle, low = bf16_terms(sketch)
    for k, term in enumerate((high, middle, low)):
        sketch_t_ref[k * width : (k + 1) * width, :] = term.T
    with_high = contract(sketch_t_ref[...], high, 1, 0)
    mixed = with_high[width : 2 * width] + with_high[2 * width :]
    middles = contract(sketch_t_ref[width : 2 * width, :], middle, 1, 0)
    gram = with_high[:width] + ((mixed + mixed.T) + middles)
    for k in range(blocks):
        left_ref[k * rows : (k + 1) * rows, :] = widened(row_ref[k], scale, 2.0 * scale, True).T
    starts = list(range(0, col_ref.shape[1], chunk))
    pending, done = [], 0

    def finish_pending():
        for c, tile in pending:
            product = contract(sketch_t_ref[: 2 * width, :], tile, 1, 0)
            for ref, term in zip(term_refs, bf16_terms(product[:width] + product[width:])):
                ref[:, c : c + chunk] = term
        pending.clear()

    def projected_until(share):
        nonlocal done
        upto = int(len(starts) * share)
        for c in starts[done:upto]:
            finish_pending()
            tile = exponent(left_ref[...], widened(col_ref[:, c : c + chunk], scale, 1.0, False))
            pending.append((c, tile))
        done = upto
        if share == 1.0:
            finish_pending()

    for t, tile in enumerate(inverse_factor(gram, projected_until)):
        inverse_ref[8 * t : 8 * t + 8, :] = tile
    left_basis_ref[...] = contract(sketch_ref[:rows, :], inverse_ref[...], 1, 1, EXACT) * norm
    count = keep_ref.shape[0]
    mine = [inverse_ref[pl.ds(pl.multiple_of(rank_ref[k] * count, count), count), :] for k in range(2)]
    terms = bf16_terms(jnp.concatenate(mine, axis=0))
    for c in range(0, col_ref.shape[1], 2 * chunk):
        at = slice(c, c + 2 * chunk)
        total = None
        for k, ref in enumerate(term_refs):
            stack = jnp.concatenate(terms[: 3 - k], axis=0)
            product = contract(stack, ref[:, at], 1, 0)
            for j in range(3 - k):
                piece = product[2 * count * j : 2 * count * (j + 1)]
                total = piece if total is None else total + piece
        keep_ref[:, at] = total[:count].astype(BF16)
        send_ref[:, at] = total[count:].astype(BF16)


def finish(index, sketch, row_blocks, col_points):
    total, width = sketch.shape
    blocks, dim, rows = row_blocks.shape
    col_dev = col_points.shape[1]
    part = jax.ShapeDtypeStruct((width // blocks, col_dev), BF16)
    whole = pl.BlockSpec(memory_space=pltpu.VMEM)
    return pl.pallas_call(
        functools.partial(finish_body, 2.0 / dim, math.sqrt(total), math.gcd(col_dev, CHUNK)),
        in_specs=[pl.BlockSpec(memory_space=pltpu.SMEM), whole, whole, whole],
        out_specs=[whole, whole, whole],
        out_shape=[jax.ShapeDtypeStruct((rows, width), F32), part, part],
        scratch_shapes=[
            pltpu.VMEM((width, width), F32),
            pltpu.VMEM((total, dim + 16), BF16),
            pltpu.VMEM((3 * width, total), BF16),
            *[pltpu.VMEM((width, col_dev), BF16)] * 3,
        ],
        compiler_params=pltpu.CompilerParams(vmem_limit_bytes=VMEM_BYTES),
        name="finish",
    )(index, sketch, row_blocks, col_points)


def place_body(at_ref, part_ref, *refs):
    out_hbm, sem = refs[-2:]
    width = part_ref.shape[1]
    at = pl.ds(pl.multiple_of(at_ref[0] * width, width), width)
    copy = pltpu.make_async_copy(part_ref, out_hbm.at[:, at], sem)
    copy.start()
    copy.wait()


def placed(part, at, out=None):
    count, width = part.shape
    remote = pl.BlockSpec(memory_space=pltpu.HBM)
    specs = [pl.BlockSpec(memory_space=pltpu.SMEM), pl.BlockSpec(memory_space=pltpu.VMEM)]
    operands = [at.reshape(1), part]
    if out is not None:
        specs.append(remote)
        operands.append(out)
    return pl.pallas_call(
        place_body,
        in_specs=specs,
        out_specs=remote,
        out_shape=jax.ShapeDtypeStruct((count, 2 * width), part.dtype),
        scratch_shapes=[pltpu.SemaphoreType.DMA],
        input_output_aliases={} if out is None else {2: 0},
        compiler_params=pltpu.CompilerParams(vmem_limit_bytes=VMEM_BYTES),
        cost_estimate=pl.CostEstimate(flops=0, bytes_accessed=4 * count * width, transcendentals=0),
        name="placed",
    )(*operands)


def swapped(value, row_bit, col_bit):
    rows, cols = lax.axis_size("row"), lax.axis_size("col")
    pairs = [(r * cols + c, (r ^ row_bit) * cols + (c ^ col_bit)) for r in range(rows) for c in range(cols)]
    return lax.ppermute(value, ("row", "col"), pairs)


def bits_up(size):
    return [1 << k for k in range(size.bit_length() - 1)]


def per_device(row_points, col_points, random_panel):
    core_bit, *y_bits = bits_up(lax.axis_size("row"))
    x_bit, *z_bits = bits_up(lax.axis_size("col"))
    half = lax.axis_index("col") % 2
    keep, send = sketch_halves(row_points, col_points, random_panel, half.reshape(1))

    def both(a, b, axis=0):
        return jnp.concatenate([a, b], axis=axis)

    def ordered(mine, other, axis=0):
        return both(jnp.where(half == 0, mine, other), jnp.where(half == 0, other, mine), axis)

    part = keep + swapped(send, 0, x_bit)
    part, col_points = lax.optimization_barrier((part, col_points))
    y_bit = y_bits[-1]
    for k, bit in enumerate(z_bits):
        if k == 0:
            row_points, part = lax.optimization_barrier((row_points, part))
            y_points = swapped(row_points, core_bit | y_bit, 0)
        moved = swapped(part, 0, bit)
        if k == 1:
            moved, y_points = lax.optimization_barrier((moved, y_points))
        part = part + moved

    far = swapped(part, core_bit | y_bit, 0)
    cross = swapped(part, y_bit, x_bit)
    near = swapped(part, core_bit, x_bit)
    split = part.shape[0]
    held, held_points = jnp.concatenate([part, near, far, cross]), jnp.stack([row_points, y_points])
    there, there_points = swapped(held, core_bit, 0), swapped(held_points, core_bit, 0)
    part, near, far, cross = held.reshape(4, split, -1)
    part_there, near_there, far_there, cross_there = there.reshape(4, split, -1)
    sketch = [ordered(part, near_there), ordered(part_there, near)]
    sketch += [ordered(far, cross_there), ordered(far_there, cross)]
    sketch = jnp.concatenate(sketch)
    row_blocks = jnp.stack([row_points, there_points[0], y_points, there_points[1]])
    for bit in y_bits[:-1]:
        sketch, row_blocks = [both(a, swapped(a, bit, 0)) for a in (sketch, row_blocks)]

    row_at = lax.axis_index("row")
    core = row_at % 2
    width = col_points.shape[1] // 2
    columns = lax.dynamic_slice_in_dim(col_points, core * width, width, 1)
    left_basis, kept, sent = finish(jnp.stack([row_at, row_at ^ core_bit]), sketch, row_blocks, columns)
    received = swapped(sent, core_bit, 0)
    return left_basis, placed(received, 1 - core, placed(kept, core))


def solution(mesh):
    placed = (P(None, "row"), P(None, "col"), P("col", None))
    return jax.shard_map(
        per_device,
        mesh=mesh,
        in_specs=placed,
        out_specs=(P("row", None), P("row", "col")),
        check_vma=False,
    )
```

```python
import functools
import math

import jax
import jax.numpy as jnp
from jax import lax
from jax.experimental import pallas as pl
from jax.experimental.pallas import tpu as pltpu
from jax.sharding import PartitionSpec as P

F32 = jnp.float32
BF16 = jnp.bfloat16
EXACT = lax.Precision.HIGHEST
VMEM_BYTES = 40 << 20
SKETCH_VMEM_BYTES = 16 << 20
CHUNK = 512


def contract(a, b, a_dim, b_dim, precision=None):
    dims = (((a_dim,), (b_dim,)), ((), ()))
    return lax.dot_general(a, b, dims, precision=precision, preferred_element_type=F32)


def widened(points, scale, factor, first):
    wide = points.astype(F32)
    terms_sum = -scale * jnp.sum(wide * wide, axis=0, keepdims=True)
    place = lax.broadcasted_iota(jnp.int32, (16, points.shape[1]), 0)
    terms_at, ones_at = (0, 3) if first else (3, 0)
    extra = jnp.where((place >= ones_at) & (place < ones_at + 3), 1.0, 0.0)
    for k in range(3):
        term = terms_sum.astype(BF16).astype(F32)
        extra = jnp.where(place == terms_at + k, term, extra)
        terms_sum = terms_sum - term
    return jnp.concatenate([(wide * factor).astype(BF16), extra.astype(BF16)], axis=0)


def exponent(left, right):
    return jnp.exp(contract(left, right, 1, 0)).astype(BF16)


def chunk_width(col_dev):
    return math.gcd(col_dev, 1024)


def half_left(row_points, scale, half, left_ref):
    left_ref[...] = widened(row_points, scale, 2.0 * scale, True).T
    rows = left_ref.shape[0] // 2
    return left_ref[pl.ds(pl.multiple_of(half * rows, rows), rows), :]


def sketch_send_body(
    scale, half_ref, row_hbm, col_hbm, panel_hbm, send_ref, col_ref, panel_ref,
    row_ref, left_ref, tile_ref, row_sem, col_sem, panel_sem,
):
    row_copy = pltpu.make_async_copy(row_hbm, row_ref, row_sem)
    col_copy = pltpu.make_async_copy(col_hbm, col_ref, col_sem)
    panel_copy = pltpu.make_async_copy(panel_hbm, panel_ref, panel_sem)
    row_copy.start()
    col_copy.start()
    panel_copy.start()
    chunk = chunk_width(col_ref.shape[1])
    row_copy.wait()
    left = half_left(row_ref[...], scale, 1 - half_ref[0], left_ref)
    col_copy.wait()
    for c in range(0, col_ref.shape[1], chunk):
        right = widened(col_ref[:, c : c + chunk], scale, 1.0, False)
        tile_ref[:, c : c + chunk] = exponent(left, right)
    panel_copy.wait()
    send_ref[...] = contract(tile_ref[...], panel_ref[...], 1, 0)


def sketch_keep_body(scale, half_ref, row_ref, col_ref, panel_ref, keep_ref, left_ref):
    left = half_left(row_ref[...], scale, half_ref[0], left_ref)
    chunk = chunk_width(col_ref.shape[1])
    total = jnp.zeros(keep_ref.shape, F32)
    for c in range(0, col_ref.shape[1], chunk):
        tile = exponent(left, widened(col_ref[:, c : c + chunk], scale, 1.0, False))
        total = total + contract(tile, panel_ref[c : c + chunk, :], 1, 0)
    keep_ref[...] = total


def sketch_halves(row_points, col_points, panel, half):
    dim, rows = row_points.shape
    col_dev, width = panel.shape
    part = jax.ShapeDtypeStruct((rows // 2, width), F32)
    whole, remote = pl.BlockSpec(memory_space=pltpu.VMEM), pl.BlockSpec(memory_space=pltpu.HBM)
    scalar = pl.BlockSpec(memory_space=pltpu.SMEM)
    send, col_near, panel_near = pl.pallas_call(
        functools.partial(sketch_send_body, 2.0 / dim),
        in_specs=[scalar, remote, remote, remote],
        out_specs=[whole, whole, whole],
        out_shape=[
            part,
            jax.ShapeDtypeStruct((dim, col_dev), BF16),
            jax.ShapeDtypeStruct((col_dev, width), BF16),
        ],
        scratch_shapes=[
            pltpu.VMEM((dim, rows), BF16),
            pltpu.VMEM((rows, dim + 16), BF16),
            pltpu.VMEM((rows // 2, col_dev), BF16),
            pltpu.SemaphoreType.DMA,
            pltpu.SemaphoreType.DMA,
            pltpu.SemaphoreType.DMA,
        ],
        compiler_params=pltpu.CompilerParams(vmem_limit_bytes=SKETCH_VMEM_BYTES),
        name="sketch_send",
    )(half, *[pltpu.with_memory_space_constraint(a, pltpu.HBM) for a in (row_points, col_points, panel)])
    keep = pl.pallas_call(
        functools.partial(sketch_keep_body, 2.0 / dim),
        in_specs=[scalar, whole, whole, whole],
        out_specs=whole,
        out_shape=part,
        scratch_shapes=[pltpu.VMEM((rows, dim + 16), BF16)],
        compiler_params=pltpu.CompilerParams(vmem_limit_bytes=SKETCH_VMEM_BYTES),
        cost_estimate=pl.CostEstimate(
            flops=rows * col_dev * (dim + 16 + width),
            bytes_accessed=2 * col_dev * (dim + 16 + width),
            transcendentals=rows // 2 * col_dev,
        ),
        name="sketch_keep",
    )(half, row_points, col_near, panel_near)
    return keep, send


def inverse_factor(gram, after_step):
    n = gram.shape[0]
    tiles = n // 8
    left = [gram[8 * t : 8 * t + 8, :] for t in range(tiles)]
    lane = lax.broadcasted_iota(jnp.int32, (8, n), 1)
    sub = lax.broadcasted_iota(jnp.int32, (8, n), 0)
    right = [jnp.where(lane == sub + 8 * t, 1.0, 0.0) for t in range(tiles)]
    inverse = []

    def row(tile, k):
        return jnp.broadcast_to(tile[k : k + 1, :], (8, n))

    def column(tile, k):
        return jnp.broadcast_to(tile[:, k : k + 1], (8, n))

    def weighted(weights, rows):
        pairs = [w * r for w, r in zip(weights, rows)]
        while len(pairs) > 1:
            pairs = [a + b for a, b in zip(pairs[::2], pairs[1::2])]
        return pairs[0]

    for b in range(tiles):
        upper, lower = left[b], right[b]
        block = [column(upper, 8 * b + k) for k in range(8)]
        root, below = [], []
        for k in range(8):
            root.append(lax.rsqrt(row(block[k], k)))
            step = jnp.where(sub > k, block[k] * root[k], 0.0)
            below.append({j: row(step, j) for j in range(k + 1, 8)})
            for j in range(k + 1, 8):
                block[j] = block[j] - step * below[k][j]
            upper_row, lower_row = row(upper, k) * root[k], row(lower, k) * root[k]
            upper, lower = upper - step * upper_row, lower - step * lower_row
        scales = root[0]
        for k in range(1, 8):
            scales = jnp.where(sub == k, root[k], scales)
        upper, lower = upper * scales, lower * scales
        inverse.append(lower)
        after_step((b + 1) / tiles)
        upper_rows = [row(upper, k) for k in range(8)]
        lower_rows = [row(lower, k) for k in range(8)]
        for t in range(b + 1, tiles):
            entry = [column(left[t], 8 * b + k) for k in range(8)]
            for k in range(8):
                entry[k] = entry[k] * root[k]
                for j in range(k + 1, 8):
                    entry[j] = entry[j] - entry[k] * below[k][j]
            left[t] = left[t] - weighted(entry, upper_rows)
            right[t] = right[t] - weighted(entry, lower_rows)
    return inverse


def bf16_terms(x):
    high = x.astype(BF16)
    rest = x - high.astype(F32)
    middle = rest.astype(BF16)
    return high, middle, (rest - middle.astype(F32)).astype(BF16)


def finish_body(
    scale, norm, chunk, rank_ref, sketch_ref, row_ref, col_ref, left_basis_ref, keep_ref, send_ref,
    inverse_ref, left_ref, sketch_t_ref, *term_refs,
):
    blocks, _, rows = row_ref.shape
    sketch = sketch_ref[...]
    width = sketch.shape[1]
    high, middle, low = bf16_terms(sketch)
    for k, term in enumerate((high, middle, low)):
        sketch_t_ref[k * width : (k + 1) * width, :] = term.T
    with_high = contract(sketch_t_ref[...], high, 1, 0)
    mixed = with_high[width : 2 * width] + with_high[2 * width :]
    middles = contract(sketch_t_ref[width : 2 * width, :], middle, 1, 0)
    gram = with_high[:width] + ((mixed + mixed.T) + middles)
    for k in range(blocks):
        left_ref[k * rows : (k + 1) * rows, :] = widened(row_ref[k], scale, 2.0 * scale, True).T
    starts = list(range(0, col_ref.shape[1], chunk))
    pending, done = [], 0

    def finish_pending():
        for c, tile in pending:
            product = contract(sketch_t_ref[: 2 * width, :], tile, 1, 0)
            for ref, term in zip(term_refs, bf16_terms(product[:width] + product[width:])):
                ref[:, c : c + chunk] = term
        pending.clear()

    def projected_until(share):
        nonlocal done
        upto = int(len(starts) * share)
        for c in starts[done:upto]:
            finish_pending()
            tile = exponent(left_ref[...], widened(col_ref[:, c : c + chunk], scale, 1.0, False))
            pending.append((c, tile))
        done = upto
        if share == 1.0:
            finish_pending()

    for t, tile in enumerate(inverse_factor(gram, projected_until)):
        inverse_ref[8 * t : 8 * t + 8, :] = tile
    left_basis_ref[...] = contract(sketch_ref[:rows, :], inverse_ref[...], 1, 1, EXACT) * norm
    count = keep_ref.shape[0]
    mine = [inverse_ref[pl.ds(pl.multiple_of(rank_ref[k] * count, count), count), :] for k in range(2)]
    terms = bf16_terms(jnp.concatenate(mine, axis=0))
    for c in range(0, col_ref.shape[1], 2 * chunk):
        at = slice(c, c + 2 * chunk)
        total = None
        for k, ref in enumerate(term_refs):
            stack = jnp.concatenate(terms[: 3 - k], axis=0)
            product = contract(stack, ref[:, at], 1, 0)
            for j in range(3 - k):
                piece = product[2 * count * j : 2 * count * (j + 1)]
                total = piece if total is None else total + piece
        keep_ref[:, at] = total[:count].astype(BF16)
        send_ref[:, at] = total[count:].astype(BF16)


def finish(index, sketch, row_blocks, col_points):
    total, width = sketch.shape
    blocks, dim, rows = row_blocks.shape
    col_dev = col_points.shape[1]
    part = jax.ShapeDtypeStruct((width // blocks, col_dev), BF16)
    whole = pl.BlockSpec(memory_space=pltpu.VMEM)
    return pl.pallas_call(
        functools.partial(finish_body, 2.0 / dim, math.sqrt(total), math.gcd(col_dev, CHUNK)),
        in_specs=[pl.BlockSpec(memory_space=pltpu.SMEM), whole, whole, whole],
        out_specs=[whole, whole, whole],
        out_shape=[jax.ShapeDtypeStruct((rows, width), F32), part, part],
        scratch_shapes=[
            pltpu.VMEM((width, width), F32),
            pltpu.VMEM((total, dim + 16), BF16),
            pltpu.VMEM((3 * width, total), BF16),
            *[pltpu.VMEM((width, col_dev), BF16)] * 3,
        ],
        compiler_params=pltpu.CompilerParams(vmem_limit_bytes=VMEM_BYTES),
        name="finish",
    )(index, sketch, row_blocks, col_points)


def place_body(at_ref, part_ref, *refs):
    out_hbm, sem = refs[-2:]
    width = part_ref.shape[1]
    at = pl.ds(pl.multiple_of(at_ref[0] * width, width), width)
    copy = pltpu.make_async_copy(part_ref, out_hbm.at[:, at], sem)
    copy.start()
    copy.wait()


def placed(part, at, out=None):
    count, width = part.shape
    remote = pl.BlockSpec(memory_space=pltpu.HBM)
    specs = [pl.BlockSpec(memory_space=pltpu.SMEM), pl.BlockSpec(memory_space=pltpu.VMEM)]
    operands = [at.reshape(1), part]
    if out is not None:
        specs.append(remote)
        operands.append(out)
    return pl.pallas_call(
        place_body,
        in_specs=specs,
        out_specs=remote,
        out_shape=jax.ShapeDtypeStruct((count, 2 * width), part.dtype),
        scratch_shapes=[pltpu.SemaphoreType.DMA],
        input_output_aliases={} if out is None else {2: 0},
        compiler_params=pltpu.CompilerParams(vmem_limit_bytes=VMEM_BYTES),
        cost_estimate=pl.CostEstimate(flops=0, bytes_accessed=4 * count * width, transcendentals=0),
        name="placed",
    )(*operands)


def swapped(value, row_bit, col_bit):
    rows, cols = lax.axis_size("row"), lax.axis_size("col")
    pairs = [(r * cols + c, (r ^ row_bit) * cols + (c ^ col_bit)) for r in range(rows) for c in range(cols)]
    return lax.ppermute(value, ("row", "col"), pairs)


def bits_up(size):
    return [1 << k for k in range(size.bit_length() - 1)]


def per_device(row_points, col_points, random_panel):
    core_bit, *y_bits = bits_up(lax.axis_size("row"))
    x_bit, *z_bits = bits_up(lax.axis_size("col"))
    half = lax.axis_index("col") % 2
    keep, send = sketch_halves(row_points, col_points, random_panel, half.reshape(1))

    def both(a, b, axis=0):
        return jnp.concatenate([a, b], axis=axis)

    def ordered(mine, other, axis=0):
        return both(jnp.where(half == 0, mine, other), jnp.where(half == 0, other, mine), axis)

    part = keep + swapped(send, 0, x_bit)
    part, col_points = lax.optimization_barrier((part, col_points))
    y_bit = y_bits[-1]
    for k, bit in enumerate(z_bits):
        if k == 0:
            row_points, part = lax.optimization_barrier((row_points, part))
            y_points = swapped(row_points, core_bit | y_bit, 0)
        moved = swapped(part, 0, bit)
        if k == 1:
            moved, y_points = lax.optimization_barrier((moved, y_points))
        part = part + moved

    far = swapped(part, y_bit, 0)
    cross = swapped(part, core_bit | y_bit, x_bit)
    near = swapped(part, core_bit, x_bit)
    split = part.shape[0]
    held, held_points = jnp.concatenate([part, near, far, cross]), jnp.stack([row_points, y_points])
    there, there_points = swapped(held, core_bit, 0), swapped(held_points, core_bit, 0)
    part, near, far, cross = held.reshape(4, split, -1)
    part_there, near_there, far_there, cross_there = there.reshape(4, split, -1)
    sketch = [ordered(part, near_there), ordered(part_there, near)]
    sketch += [ordered(far, cross_there), ordered(far_there, cross)]
    sketch = jnp.concatenate(sketch)
    row_blocks = jnp.stack([row_points, there_points[0], there_points[1], y_points])
    for bit in y_bits[:-1]:
        sketch, row_blocks = [both(a, swapped(a, bit, 0)) for a in (sketch, row_blocks)]

    row_at = lax.axis_index("row")
    core = row_at % 2
    width = col_points.shape[1] // 2
    columns = lax.dynamic_slice_in_dim(col_points, core * width, width, 1)
    left_basis, kept, sent = finish(jnp.stack([row_at, row_at ^ core_bit]), sketch, row_blocks, columns)
    received = swapped(sent, core_bit, 0)
    return left_basis, placed(received, 1 - core, placed(kept, core))


def solution(mesh):
    placed = (P(None, "row"), P(None, "col"), P("col", None))
    return jax.shard_map(
        per_device,
        mesh=mesh,
        in_specs=placed,
        out_specs=(P("row", None), P("row", "col")),
        check_vma=False,
    )
```
